32 devices in a mesh: space: 8 (over y, x, core), orb: 4 (over z).
Axes of the slice: x: 2, y: 2, z: 4, core: 2. Of those that a mesh axis runs over, the one named last changes fastest.
Arguments:
- wavefunctions: float32 [8, 1536, 384], P('space', None, 'orb'), may hold values from -70 to 70
- cell_ham: float32 [8, 4, 729, 729], P('space'), may hold values from -1 to 1, as said below
- cell_nodes: int32 [8, 4, 729], P('space'), may hold values from 0 to 1535, as said below
- cell_count: int32 [8], P('space'), may hold values from 2 to 4, as said below
- upper_nodes: int32 [8, 512], P('space'), may hold values from 0 to 1536, as said below
- lower_nodes: int32 [8, 512], P('space'), may hold values from 0 to 1536, as said below
Outputs:
- rotated: float32 [8, 1536, 384], P('space', 'orb')
The draws below stay inside these ranges and needn't reach their ends.
Inputs may be any that keep to these rules, and one draw needn't show every extreme that they name: `cell_nodes`: each cell's 729 entries are distinct. `cell_count`: some part has 4 live cells. Entries equal to 1536 are empty slots and come after the live ones; for p < 7, upper_nodes[p, k] is live exactly where lower_nodes[p + 1, k] is, and the two name the same shared node; the live entries of upper_nodes[p] and lower_nodes[p] are all distinct; the last part's list is empty; some list has all 512 slots live. `lower_nodes`: paired with upper_nodes as stated there; the first part's list is empty. `cell_ham`: each cell's matrix is symmetric.
All inputs are finite; a program needn't handle non-finite values.
Results may differ from the reference program's by a relative error of at most 0.0003.
Values sent between devices are 32-bit elements; how exact they have to be, the bound alone decides.
A program may use at most 64 MiB of HBM per device.

```python
import math
import jax
import jax.numpy as jnp
from jax import lax

COLS = 384
CELL_NODES = 729
CAP = 4
NODES_DEV = 1536
DEGREE = 3
SHARE = 512
N_SPACE = 8


def draw_wavefunctions(key, part):
    key_base, key_node, key_column = jax.random.split(key, 3)
    device_rank = jnp.arange(N_SPACE, dtype=jnp.float32)
    amplitude = jnp.sqrt(1.0 + 2.0 * device_rank / max(N_SPACE - 1, 1))[:, None, None]
    node_scale = jnp.exp(jax.random.uniform(key_node, (N_SPACE, NODES_DEV, 1), jnp.float32, math.log(0.5), math.log(5.0)))
    column_scale = jnp.exp(jax.random.uniform(key_column, (1, 1, COLS), jnp.float32, math.log(0.5), math.log(2.0)))
    entries = jnp.clip(jax.random.normal(key_base, (N_SPACE, NODES_DEV, COLS), jnp.float32), -4.0, 4.0)
    return entries * amplitude * node_scale * column_scale


def draw_cell_ham(key, part):
    subkeys = jax.random.split(key, N_SPACE)

    def one_device(device_key):
        entries = jnp.clip(jax.random.normal(device_key, (CAP, CELL_NODES, CELL_NODES), jnp.float32), -4.0, 4.0)
        return (entries + jnp.swapaxes(entries, 1, 2)) * (0.5 / math.sqrt(2.0 * CELL_NODES))
    return lax.map(one_device, subkeys)


def draw_cell_nodes(key, part):
    subkeys = jax.random.split(key, N_SPACE * CAP)
    orderings = jax.vmap(lambda cell_key: jax.random.permutation(cell_key, NODES_DEV)[:CELL_NODES])(subkeys)
    return orderings.reshape(N_SPACE, CAP, CELL_NODES).astype(jnp.int32)


def draw_cell_count(key, part):
    key_count, key_chosen = jax.random.split(key, 2)
    counts = jax.random.randint(key_count, (N_SPACE,), CAP // 2, CAP + 1, jnp.int32)
    chosen = jax.random.randint(key_chosen, (), 0, N_SPACE, jnp.int32)
    return counts.at[chosen].set(CAP).astype(jnp.int32)


def shared_lists(key):
    base_key = jax.random.fold_in(key, 11)
    key_order, key_length, key_chosen = jax.random.split(base_key, 3)
    orderings = jax.vmap(lambda device_key: jax.random.permutation(device_key, NODES_DEV))(jax.random.split(key_order, N_SPACE)).astype(jnp.int32)
    lengths = jax.random.randint(key_length, (N_SPACE,), SHARE // 2, SHARE + 1, jnp.int32)
    chosen = jax.random.randint(key_chosen, (), 0, N_SPACE - 1, jnp.int32)
    lengths = lengths.at[chosen].set(SHARE).at[N_SPACE - 1].set(0)
    lengths_below = jnp.concatenate([jnp.zeros((1,), jnp.int32), lengths[:-1]])
    slot_rank = jnp.arange(SHARE, dtype=jnp.int32)
    upper_lists = jnp.where(slot_rank[None, :] < lengths[:, None], orderings[:, :SHARE], NODES_DEV)
    lower_lists = jnp.where(slot_rank[None, :] < lengths_below[:, None], orderings[:, SHARE:2 * SHARE], NODES_DEV)
    return (upper_lists.astype(jnp.int32), lower_lists.astype(jnp.int32))


def draw_upper_nodes(key, part):
    return shared_lists(key)[0]


def draw_lower_nodes(key, part):
    return shared_lists(key)[1]


def setup_inputs(seed: int = 0) -> dict:
    keys = jax.random.split(jax.random.key(seed), 7)
    wavefunctions = draw_wavefunctions(jax.random.fold_in(keys[6], 71), 0)
    cell_ham = draw_cell_ham(jax.random.fold_in(keys[6], 71), 0)
    cell_nodes = draw_cell_nodes(jax.random.fold_in(keys[6], 71), 0)
    cell_count = draw_cell_count(jax.random.fold_in(keys[6], 71), 0)
    upper_nodes = draw_upper_nodes(jax.random.fold_in(keys[6], 71), 0)
    lower_nodes = draw_lower_nodes(jax.random.fold_in(keys[6], 71), 0)
    return {"wavefunctions": wavefunctions, "cell_ham": cell_ham, "cell_nodes": cell_nodes, "cell_count": cell_count, "upper_nodes": upper_nodes, "lower_nodes": lower_nodes}


center_shift = 0.5
half_width = 2.0

def assemble_all(nodal_field, cell_ham, cell_nodes, cell_count):

    def per_device(device_args):
        values, matrices, node_map, live_cells = device_args
        assembled = jnp.zeros_like(values)
        for cell_slot in range(CAP):
            rows = node_map[cell_slot]
            product = lax.dot_general(matrices[cell_slot].astype(jnp.float32), jnp.take(values, rows, axis=0).astype(jnp.float32), (((0,), (0,)), ((), ())), precision=lax.Precision.HIGHEST, preferred_element_type=jnp.float32)
            keep_cell = (cell_slot < live_cells).astype(jnp.float32)
            assembled = assembled.at[rows].add(product * keep_cell)
        return assembled
    return lax.map(per_device, (nodal_field, cell_ham, cell_nodes, cell_count))

def fetch_rims(values, positions):
    return values.at[positions].get(mode='fill', fill_value=0.0)

def place_rims(values, upper_list, lower_list, from_above, from_below):
    return values.at[upper_list].add(from_above, mode='drop').at[lower_list].add(from_below, mode='drop')

def operate(nodal_field, cell_ham, cell_nodes, cell_count, upper_nodes, lower_nodes):
    assembled = assemble_all(nodal_field, cell_ham, cell_nodes, cell_count)
    upper_values = jax.vmap(fetch_rims)(assembled, upper_nodes)
    lower_values = jax.vmap(fetch_rims)(assembled, lower_nodes)
    no_values = jnp.zeros_like(upper_values[:1])
    from_above = jnp.concatenate([lower_values[1:], no_values], axis=0)
    from_below = jnp.concatenate([no_values, upper_values[:-1]], axis=0)
    return jax.vmap(place_rims)(assembled, upper_nodes, lower_nodes, from_above, from_below)

def reference(wavefunctions, cell_ham, cell_nodes, cell_count, upper_nodes, lower_nodes):
    start_field = wavefunctions
    previous = start_field
    current = (operate(start_field, cell_ham, cell_nodes, cell_count, upper_nodes, lower_nodes) - center_shift * start_field) / half_width
    for repeat in range(DEGREE - 1):
        following = 2.0 * (operate(current, cell_ham, cell_nodes, cell_count, upper_nodes, lower_nodes) - center_shift * current) / half_width - previous
        previous, current = (current, following)
    weight = jax.vmap(lambda lower_list: jnp.ones((NODES_DEV,), jnp.float32).at[lower_list].set(0.0, mode='drop'))(lower_nodes)
    weight = weight * (1.0 / (N_SPACE * NODES_DEV))
    gram_total = jnp.einsum('pnc,pnd->cd', current * weight[:, :, None], current, precision=lax.Precision.HIGHEST)
    factor = jnp.linalg.cholesky(gram_total)
    filtered = current.reshape(N_SPACE * NODES_DEV, COLS)
    solved = lax.linalg.triangular_solve(factor, filtered, left_side=False, lower=True, transpose_a=True)
    return solved.reshape(N_SPACE, NODES_DEV, COLS)
```

```python
import functools

import jax
import jax.numpy as jnp
from jax import lax
from jax.experimental import pallas as pl
from jax.experimental.pallas import tpu as pltpu
from jax.sharding import PartitionSpec as P

DEGREE = 3


center_shift = 0.5
half_width = 2.0


def shifted(block, axis, distance):
    devices = range(lax.axis_size(axis))
    route = [(i - distance, i) for i in devices if i - distance in devices]
    return lax.ppermute(block, axis, route)


def assemble(nodal_field, matrices, node_map, live_cells):

    def add_cell(cell_slot, assembled):
        rows = lax.dynamic_index_in_dim(node_map, cell_slot, 0, keepdims=False)
        matrix = lax.dynamic_index_in_dim(matrices, cell_slot, 0, keepdims=False)
        product = lax.dot_general(
            matrix,
            jnp.take(nodal_field, rows, axis=0),
            (((0,), (0,)), ((), ())),
            precision=lax.Precision.HIGHEST,
            preferred_element_type=jnp.float32,
        )
        return assembled.at[rows].add(product)

    return lax.fori_loop(0, live_cells, add_cell, jnp.zeros_like(nodal_field))


def share_sums(assembled, upper_list, lower_list):
    outgoing = assembled.at[lower_list].get(mode="fill", fill_value=0.0)
    arriving = shifted(outgoing, "space", -1)
    assembled = assembled.at[upper_list].add(arriving, mode="drop")
    summed = assembled.at[upper_list].get(mode="fill", fill_value=0.0)
    returned = shifted(summed, "space", 1)
    return assembled.at[lower_list].set(returned, mode="drop")


LANES = 128
GROUP = 8
MESH = pl.DeviceIdType.MESH


def exact_dot(left, right, dims):
    return lax.dot_general(
        left,
        right,
        (dims, ((), ())),
        precision=lax.Precision.HIGHEST,
        preferred_element_type=jnp.float32,
    )


def block_pairs(blocks):
    return [(i, j) for i in range(blocks) for j in range(i + 1)]


def gram_kernel(n_space, n_orb, inside, field, lower_list, rows_out, gram_out, pieces, local, parts, slab, others,
                turn_send, turn_recv, split_send, split_recv, orb_send, orb_recv, join_send, join_recv):
    space, orb = lax.axis_index("space"), lax.axis_index("orb")
    node_total, width = field.shape
    quarter = node_total // n_orb
    columns = width * n_orb
    partners = n_orb - 1

    barrier = pltpu.get_barrier_semaphore()
    for step in range(1, n_orb):
        pl.semaphore_signal(barrier, inc=1, device_id={"orb": lax.rem(orb + step, n_orb)}, device_id_type=MESH)
    if inside:
        partners += n_space - 1
        for step in range(1, n_space):
            pl.semaphore_signal(barrier, inc=1, device_id={"space": lax.rem(space + step, n_space)}, device_id_type=MESH)
    pl.semaphore_wait(barrier, partners)

    def exchange(axis, size, here, send_sems, recv_sems, source, target):
        copies = []
        for step in range(1, size):
            other = lax.rem(here + step, size)
            copy = pltpu.make_async_remote_copy(
                src_ref=source(other),
                dst_ref=target,
                send_sem=send_sems.at[step],
                recv_sem=recv_sems.at[step],
                device_id={axis: other},
                device_id_type=MESH,
            )
            copy.start()
            copies.append(copy)
        return copies

    def own_quarter(which):
        return field.at[pl.ds(pl.multiple_of(which * quarter, 8), quarter)]

    copies = exchange("orb", n_orb, orb, turn_send, turn_recv, own_quarter, pieces.at[orb])
    pieces[orb] = field[pl.ds(pl.multiple_of(orb * quarter, 8), quarter), :]
    node = lax.broadcasted_iota(jnp.int32, (quarter, lower_list.shape[1]), 0) + orb * quarter
    hits = jnp.where(node == lower_list[...], 1.0, 0.0)
    weight = (1.0 - jnp.max(hits, axis=1, keepdims=True)) * (1.0 / (n_space * node_total))
    for copy in copies:
        copy.wait()
    for which in range(n_orb):
        rows_out[:, which * width : (which + 1) * width] = pieces[which]

    blocks = columns // LANES
    for spot, (i, j) in enumerate(block_pairs(blocks)):
        left = rows_out[:, i * LANES : (i + 1) * LANES] * weight
        right = rows_out[:, j * LANES : (j + 1) * LANES]
        term = exact_dot(left, right, ((0,), (0,)))
        if inside:
            local[spot * LANES : (spot + 1) * LANES, :] = term
        else:
            gram_out[spot * LANES : (spot + 1) * LANES, :] = term
    if not inside:
        return

    chunk = local.shape[0] // n_space

    def chunk_of(which):
        return local.at[pl.ds(pl.multiple_of(which * chunk, 8), chunk)]

    copies = exchange("space", n_space, space, split_send, split_recv, chunk_of, parts.at[space])
    parts[space] = local[pl.ds(pl.multiple_of(space * chunk, 8), chunk), :]
    for copy in copies:
        copy.wait()
    slab[...] = jnp.sum(parts[...], axis=0)

    copies = exchange("orb", n_orb, orb, orb_send, orb_recv, lambda _: slab, others.at[orb])
    others[orb] = slab[...]
    for copy in copies:
        copy.wait()
    mine = pl.ds(pl.multiple_of(space * chunk, 8), chunk)
    gram_out[mine, :] = jnp.sum(others[...], axis=0)
    copies = exchange("space", n_space, space, join_send, join_recv, lambda _: gram_out.at[mine], gram_out.at[mine])
    for copy in copies:
        copy.wait()


def turn_and_gram(field, lower_list, n_space, n_orb):
    node_total, width = field.shape
    quarter, columns = node_total // n_orb, width * n_orb
    packed = len(block_pairs(columns // LANES)) * LANES
    inside = n_space <= 8 and packed % (8 * n_space) == 0
    groups = n_space if inside else 1
    chunk = packed // groups
    dma = pltpu.SemaphoreType.DMA
    vmem = pl.BlockSpec(memory_space=pltpu.VMEM)
    rows, gram = pl.pallas_call(
        functools.partial(gram_kernel, n_space, n_orb, inside),
        out_shape=(
            jax.ShapeDtypeStruct((quarter, columns), jnp.float32),
            jax.ShapeDtypeStruct((packed, LANES), jnp.float32),
        ),
        in_specs=[vmem, vmem],
        out_specs=(vmem, vmem),
        scratch_shapes=[
            pltpu.VMEM((n_orb, quarter, width), jnp.float32),
            pltpu.VMEM((packed, LANES), jnp.float32),
            pltpu.VMEM((groups, chunk, LANES), jnp.float32),
            pltpu.VMEM((chunk, LANES), jnp.float32),
            pltpu.VMEM((n_orb, chunk, LANES), jnp.float32),
            dma((n_orb,)), dma((n_orb,)),
            dma((groups,)), dma((groups,)),
            dma((n_orb,)), dma((n_orb,)),
            dma((groups,)), dma((groups,)),
        ],
        compiler_params=pltpu.CompilerParams(
            collective_id=1, has_side_effects=True, vmem_limit_bytes=40 * 2**20
        ),
        name="turn_and_gram",
    )(field, lower_list)
    if not inside:
        gram = lax.psum(gram, ("space", "orb"))
    return rows, gram


def invert_factor(matrix, inverse):
    size = matrix.shape[0]
    row_id = lax.broadcasted_iota(jnp.int32, (size, size), 0)
    column_id = lax.broadcasted_iota(jnp.int32, (size, size), 1)
    inverse[...] = jnp.where(row_id == column_id, 1.0, 0.0)
    for start in range(0, size, GROUP):
        below = start + GROUP
        rows = [matrix[start + b : start + b + 1, :] for b in range(GROUP)]
        eyes = [inverse[start + b : start + b + 1, :] for b in range(GROUP)]
        entry = {
            (b, c): jnp.broadcast_to(rows[b][:, start + c : start + c + 1], (1, size))
            for b in range(GROUP)
            for c in range(b + 1)
        }
        lower, scale, done = {}, [], []
        for b in range(GROUP):
            scale.append(lax.rsqrt(entry[b, b]))
            for i in range(b + 1, GROUP):
                lower[i, b] = entry[i, b] * scale[b]
            for i in range(b + 1, GROUP):
                for j in range(b + 1, i + 1):
                    entry[i, j] = entry[i, j] - lower[i, b] * lower[j, b]
            done.append((rows[b] * scale[b], eyes[b] * scale[b]))
            for i in range(b + 1, GROUP):
                rows[i] = rows[i] - lower[i, b] * done[b][0]
                eyes[i] = eyes[i] - lower[i, b] * done[b][1]
        for b in range(GROUP):
            inverse[start + b : start + b + 1, :] = done[b][1]
        if below == size:
            break
        back = list(done)
        for b in reversed(range(GROUP)):
            back[b] = (back[b][0] * scale[b], back[b][1] * scale[b])
            for i in range(b):
                back[i] = (back[i][0] - lower[b, i] * back[b][0], back[i][1] - lower[b, i] * back[b][1])
        rest = matrix[below:, :]
        rest_eye = inverse[below:, :]
        raw = [jnp.broadcast_to(rest[:, start + c : start + c + 1], rest.shape) for c in range(GROUP)]
        for c in range(GROUP):
            rest = rest - raw[c] * back[c][0]
            rest_eye = rest_eye - raw[c] * back[c][1]
        matrix[below:, :] = rest
        inverse[below:, :] = rest_eye


def rotate_kernel(rows, gram, rotated, lower, block, inverse):
    columns = rows.shape[1]
    blocks = columns // LANES
    lower[...] = jnp.zeros_like(lower)
    rotated[...] = jnp.zeros_like(rotated)
    last, second = ((1,), (1,)), ((1,), (1,))

    def one_block(k, carry):
        here = pl.ds(pl.multiple_of(k * LANES, LANES), LANES)
        spot = (k * (k + 3)) // 2
        own = lower[k]
        diagonal = gram[pl.ds(pl.multiple_of(spot * LANES, LANES), LANES), :]
        block[...] = diagonal - exact_dot(own, own, last)
        invert_factor(block, inverse)
        for i in range(1, blocks):

            @pl.when(i > k)
            def _():
                at = (i * (i + 1)) // 2 + k
                under = gram[pl.ds(pl.multiple_of(at * LANES, LANES), LANES), :]
                under = under - exact_dot(lower[i], own, last)
                lower[i, :, here] = exact_dot(under, inverse[...], second)

        left = rows[:, here] - exact_dot(rotated[...], own, last)
        rotated[:, here] = exact_dot(left, inverse[...], second)
        return carry

    lax.fori_loop(0, blocks, one_block, 0)


def rotate(rows, gram):
    columns = rows.shape[1]
    vmem = pl.BlockSpec(memory_space=pltpu.VMEM)
    return pl.pallas_call(
        rotate_kernel,
        out_shape=jax.ShapeDtypeStruct(rows.shape, jnp.float32),
        in_specs=[vmem, vmem],
        out_specs=vmem,
        scratch_shapes=[
            pltpu.VMEM((columns // LANES, LANES, columns), jnp.float32),
            pltpu.VMEM((LANES, LANES), jnp.float32),
            pltpu.VMEM((LANES, LANES), jnp.float32),
        ],
        compiler_params=pltpu.CompilerParams(vmem_limit_bytes=40 * 2**20),
        name="rotate",
    )(rows, gram)


def shards(wavefunctions, cell_ham, cell_nodes, cell_count, upper_nodes, lower_nodes):
    start_field = wavefunctions[0]
    matrices = cell_ham[0]
    node_map = cell_nodes[0]
    live_cells = cell_count[0]
    upper_list = upper_nodes[0]
    lower_list = lower_nodes[0]

    def operate(nodal_field):
        return share_sums(
            assemble(nodal_field, matrices, node_map, live_cells), upper_list, lower_list
        )

    previous = start_field
    current = (operate(start_field) - center_shift * start_field) / half_width
    for repeat in range(DEGREE - 1):
        following = 2.0 * (operate(current) - center_shift * current) / half_width - previous
        previous, current = (current, following)
    rows, gram = turn_and_gram(current, lower_nodes, lax.axis_size("space"), lax.axis_size("orb"))
    return rotate(rows, gram)[None]


def solution(mesh):
    in_specs = (
        P("space", None, "orb"),
        P("space", None, None, None),
        P("space", None, None),
        P("space"),
        P("space", None),
        P("space", None),
    )
    out_specs = P("space", "orb", None)
    return jax.shard_map(shards, mesh=mesh, in_specs=in_specs, out_specs=out_specs, check_vma=False)
```

```python
import functools

import jax
import jax.numpy as jnp
from jax import lax
from jax.experimental import pallas as pl
from jax.experimental.pallas import tpu as pltpu
from jax.sharding import PartitionSpec as P

DEGREE = 3
LANES = 128
GROUP = 8
MESH = pl.DeviceIdType.MESH


center_shift = 0.5
half_width = 2.0


def split(values):
    high = values.astype(jnp.bfloat16)
    return high, (values - high.astype(jnp.float32)).astype(jnp.bfloat16)


def plain_dot(left, right):
    return lax.dot_general(left, right, (((1,), (0,)), ((), ())), preferred_element_type=jnp.float32)


def folded(product):
    return product[:, :LANES] + product[:, LANES:]


def filter_kernel(n_space, degree, start, matrices, node_row, list_row, out, gather, scatter, pick, place, stack,
                  fields, packed, cell_out, sums, outgoing, arriving, load_sem, send_sem, recv_sem):
    space = lax.axis_index("space")
    nodes, width = start.shape
    cells, doubled, cell_size = stack.shape
    slots = list_row.shape[1] // 2
    has_above, has_below = space < n_space - 1, space > 0

    for cell in range(cells):
        pltpu.make_async_copy(matrices.at[cell], stack.at[cell], load_sem.at[cell]).start()
    arriving[...] = jnp.zeros_like(arriving)

    barrier = pltpu.get_barrier_semaphore()

    @pl.when(has_above)
    def _():
        pl.semaphore_signal(barrier, inc=1, device_id={"space": space + 1}, device_id_type=MESH)

    @pl.when(has_below)
    def _():
        pl.semaphore_signal(barrier, inc=1, device_id={"space": space - 1}, device_id_type=MESH)

    lane = lax.broadcasted_iota(jnp.int32, (LANES, LANES), 1).astype(jnp.float32)
    sublane = lax.broadcasted_iota(jnp.int32, (LANES, LANES), 0).astype(jnp.float32)

    def ones_where(condition):
        return jnp.where(condition, 1.0, 0.0).astype(jnp.bfloat16)

    def tile_at(index):
        return pl.ds(pl.multiple_of(index * LANES, LANES), LANES)

    def upright(row):
        return jnp.transpose(jnp.broadcast_to(row, (LANES, LANES)))

    def gather_rows(chunk, carry):
        here = tile_at(chunk)
        column = upright(node_row[:, here])
        for tile in range(nodes // LANES):
            gather[here, tile * LANES : (tile + 1) * LANES] = ones_where(column == lane + float(tile * LANES))
        return carry

    def pick_rows(chunk, carry):
        here = tile_at(chunk)
        column = upright(list_row[:, here])
        for tile in range(node_row.shape[1] // LANES):
            there = slice(tile * LANES, (tile + 1) * LANES)
            pick[here, there] = ones_where(column == node_row[:, there])
        return carry

    def node_rows(chunk, carry):
        here = tile_at(chunk)
        node = sublane + (chunk * LANES).astype(jnp.float32)
        for tile in range(node_row.shape[1] // LANES):
            there = slice(tile * LANES, (tile + 1) * LANES)
            scatter[here, there] = ones_where(node == node_row[:, there])
        for tile in range(2 * slots // LANES):
            there = slice(tile * LANES, (tile + 1) * LANES)
            other = (tile * LANES + slots) % (2 * slots)
            place[here, there] = ones_where(node == list_row[:, other : other + LANES])
        values = jnp.concatenate([start[here, :], jnp.zeros((LANES, LANES - width), jnp.float32)], axis=1)
        fields[0, here, :] = values
        fields[1, here, :] = values
        high, low = split(values)
        packed[here, :LANES] = high
        packed[here, LANES:] = low
        return carry

    lax.fori_loop(0, node_row.shape[1] // LANES, gather_rows, 0)
    lax.fori_loop(0, 2 * slots // LANES, pick_rows, 0)
    lax.fori_loop(0, nodes // LANES, node_rows, 0)
    for cell in range(cells):
        pltpu.make_async_copy(matrices.at[cell], stack.at[cell], load_sem.at[cell]).wait()
    pl.semaphore_wait(barrier, has_above.astype(jnp.int32) + has_below.astype(jnp.int32))

    part = nodes // 3 if nodes % (3 * LANES) == 0 else LANES

    def apply(step, carry):
        def one_cell(cell, carry):
            here = pl.ds(pl.multiple_of(cell * cell_size, LANES), cell_size)
            local = plain_dot(gather[here, :], packed[...]).astype(jnp.bfloat16)
            high_part = plain_dot(stack[cell, :cell_size, :], local)
            low_part = plain_dot(stack[cell, cell_size:, :], local[:, :LANES])
            high, low = split(folded(high_part) + low_part)
            cell_out[here, :LANES] = high
            cell_out[here, LANES:] = low
            return carry

        lax.fori_loop(0, cells, one_cell, 0)

        def transfer(way, towards):
            return pltpu.make_async_remote_copy(
                src_ref=outgoing.at[way],
                dst_ref=arriving.at[step, way],
                send_sem=send_sem.at[step, way],
                recv_sem=recv_sem.at[step, way],
                device_id={"space": towards},
                device_id_type=MESH,
            )

        down, up = transfer(0, space - 1), transfer(1, space + 1)
        outgoing[0] = folded(plain_dot(pick[:slots, :], cell_out[...]))

        @pl.when(has_below)
        def _():
            down.start()

        outgoing[1] = folded(plain_dot(pick[slots:, :], cell_out[...]))

        @pl.when(has_above)
        def _():
            up.start()

        def node_sums(chunk, carry):
            here = pl.ds(pl.multiple_of(chunk * part, LANES), part)
            sums[here, :] = folded(plain_dot(scatter[here, :], cell_out[...]))
            return carry

        lax.fori_loop(0, nodes // part, node_sums, 0)

        @pl.when(has_below)
        def _():
            down.wait_send()
            up.wait_recv()

        @pl.when(has_above)
        def _():
            up.wait_send()
            down.wait_recv()

        new, old = lax.rem(step + 1, 2), lax.rem(step, 2)
        first = step == 0
        scale = jnp.where(first, 1.0 / half_width, 2.0 / half_width)
        keep = jnp.where(first, 0.0, 1.0)
        parts = [split(arriving[step, way]) for way in range(2)]
        arrived = jnp.concatenate([jnp.concatenate(pair, axis=1) for pair in parts], axis=0)

        def advance(chunk, carry):
            here = pl.ds(pl.multiple_of(chunk * part, LANES), part)
            total = sums[here, :] + folded(plain_dot(place[here, :], arrived))
            value = scale * (total - center_shift * fields[old, here, :]) - keep * fields[new, here, :]
            fields[new, here, :] = value
            high, low = split(value)
            packed[here, :LANES] = high
            packed[here, LANES:] = low
            return carry

        lax.fori_loop(0, nodes // part, advance, 0)
        return carry

    lax.fori_loop(0, degree, apply, 0)
    out[...] = fields[degree % 2, :, :width]


def filtered_block(start, matrices, node_map, live_cells, upper_list, lower_list, n_space):
    nodes, width = start.shape
    cells, cell_nodes = node_map.shape
    cell_size = -(-cell_nodes // LANES) * LANES
    room = cell_size - cell_nodes
    slots = upper_list.shape[0]

    high = lax.reduce_precision(matrices, exponent_bits=8, mantissa_bits=7)
    margin = ((0, 0), (0, room), (0, room))
    stack = jnp.concatenate(
        [jnp.pad(piece.astype(jnp.bfloat16), margin) for piece in (high, matrices - high)], axis=1
    )
    live = jnp.arange(cells)[:, None] < live_cells
    node_row = jnp.pad(jnp.where(live, node_map, -1), ((0, 0), (0, room)), constant_values=-1)
    node_row = node_row.reshape(1, cells * cell_size).astype(jnp.float32)
    list_row = jnp.concatenate([lower_list, upper_list]).reshape(1, 2 * slots).astype(jnp.float32)

    vmem, anywhere = pl.BlockSpec(memory_space=pltpu.VMEM), pl.BlockSpec(memory_space=pl.ANY)
    dma = pltpu.SemaphoreType.DMA
    every, half = jnp.float32, jnp.bfloat16
    return pl.pallas_call(
        functools.partial(filter_kernel, n_space, DEGREE),
        out_shape=jax.ShapeDtypeStruct(start.shape, jnp.float32),
        in_specs=[vmem, anywhere, vmem, vmem],
        out_specs=vmem,
        scratch_shapes=[
            pltpu.VMEM((cells * cell_size, nodes), half),
            pltpu.VMEM((nodes, cells * cell_size), half),
            pltpu.VMEM((2 * slots, cells * cell_size), half),
            pltpu.VMEM((nodes, 2 * slots), half),
            pltpu.VMEM((cells, 2 * cell_size, cell_size), half),
            pltpu.VMEM((2, nodes, LANES), every),
            pltpu.VMEM((nodes, 2 * LANES), half),
            pltpu.VMEM((cells * cell_size, 2 * LANES), half),
            pltpu.VMEM((nodes, LANES), every),
            pltpu.VMEM((2, slots, LANES), every),
            pltpu.VMEM((DEGREE, 2, slots, LANES), every),
            dma((cells,)),
            dma((DEGREE, 2)),
            dma((DEGREE, 2)),
        ],
        compiler_params=pltpu.CompilerParams(
            collective_id=2, has_side_effects=True, vmem_limit_bytes=58 * 2**20
        ),
        name="filter",
    )(start, stack, node_row, list_row)


def exact_dot(left, right, dims):
    return lax.dot_general(
        left,
        right,
        (dims, ((), ())),
        precision=lax.Precision.HIGHEST,
        preferred_element_type=jnp.float32,
    )


def block_pairs(blocks):
    return [(i, j) for i in range(blocks) for j in range(i + 1)]


def gram_kernel(n_space, n_orb, inside, field, lower_list, rows_out, gram_out, pieces, local, parts, slab, others,
                turn_send, turn_recv, split_send, split_recv, orb_send, orb_recv, join_send, join_recv):
    space, orb = lax.axis_index("space"), lax.axis_index("orb")
    node_total, width = field.shape
    quarter = node_total // n_orb
    columns = width * n_orb
    partners = n_orb - 1

    barrier = pltpu.get_barrier_semaphore()
    for step in range(1, n_orb):
        pl.semaphore_signal(barrier, inc=1, device_id={"orb": lax.rem(orb + step, n_orb)}, device_id_type=MESH)
    if inside:
        partners += n_space - 1
        for step in range(1, n_space):
            pl.semaphore_signal(barrier, inc=1, device_id={"space": lax.rem(space + step, n_space)}, device_id_type=MESH)
    pl.semaphore_wait(barrier, partners)

    def exchange(axis, size, here, send_sems, recv_sems, source, target):
        copies = []
        for step in range(1, size):
            other = lax.rem(here + step, size)
            copy = pltpu.make_async_remote_copy(
                src_ref=source(other),
                dst_ref=target,
                send_sem=send_sems.at[step],
                recv_sem=recv_sems.at[step],
                device_id={axis: other},
                device_id_type=MESH,
            )
            copy.start()
            copies.append(copy)
        return copies

    def own_quarter(which):
        return field.at[pl.ds(pl.multiple_of(which * quarter, 8), quarter)]

    copies = exchange("orb", n_orb, orb, turn_send, turn_recv, own_quarter, pieces.at[orb])
    pieces[orb] = field[pl.ds(pl.multiple_of(orb * quarter, 8), quarter), :]
    node = lax.broadcasted_iota(jnp.int32, (quarter, lower_list.shape[1]), 0) + orb * quarter
    hits = jnp.where(node == lower_list[...], 1.0, 0.0)
    weight = (1.0 - jnp.max(hits, axis=1, keepdims=True)) * (1.0 / (n_space * node_total))
    for copy in copies:
        copy.wait()
    for which in range(n_orb):
        rows_out[:, which * width : (which + 1) * width] = pieces[which]

    blocks = columns // LANES
    for spot, (i, j) in enumerate(block_pairs(blocks)):
        left = rows_out[:, i * LANES : (i + 1) * LANES] * weight
        right = rows_out[:, j * LANES : (j + 1) * LANES]
        term = exact_dot(left, right, ((0,), (0,)))
        if inside:
            local[spot * LANES : (spot + 1) * LANES, :] = term
        else:
            gram_out[spot * LANES : (spot + 1) * LANES, :] = term
    if not inside:
        return

    chunk = local.shape[0] // n_space

    def chunk_of(which):
        return local.at[pl.ds(pl.multiple_of(which * chunk, 8), chunk)]

    copies = exchange("space", n_space, space, split_send, split_recv, chunk_of, parts.at[space])
    parts[space] = local[pl.ds(pl.multiple_of(space * chunk, 8), chunk), :]
    for copy in copies:
        copy.wait()
    slab[...] = jnp.sum(parts[...], axis=0)

    copies = exchange("orb", n_orb, orb, orb_send, orb_recv, lambda _: slab, others.at[orb])
    others[orb] = slab[...]
    for copy in copies:
        copy.wait()
    mine = pl.ds(pl.multiple_of(space * chunk, 8), chunk)
    gram_out[mine, :] = jnp.sum(others[...], axis=0)
    copies = exchange("space", n_space, space, join_send, join_recv, lambda _: gram_out.at[mine], gram_out.at[mine])
    for copy in copies:
        copy.wait()


def turn_and_gram(field, lower_list, n_space, n_orb):
    node_total, width = field.shape
    quarter, columns = node_total // n_orb, width * n_orb
    packed = len(block_pairs(columns // LANES)) * LANES
    inside = n_space <= 8 and packed % (8 * n_space) == 0
    groups = n_space if inside else 1
    chunk = packed // groups
    dma = pltpu.SemaphoreType.DMA
    vmem = pl.BlockSpec(memory_space=pltpu.VMEM)
    rows, gram = pl.pallas_call(
        functools.partial(gram_kernel, n_space, n_orb, inside),
        out_shape=(
            jax.ShapeDtypeStruct((quarter, columns), jnp.float32),
            jax.ShapeDtypeStruct((packed, LANES), jnp.float32),
        ),
        in_specs=[vmem, vmem],
        out_specs=(vmem, vmem),
        scratch_shapes=[
            pltpu.VMEM((n_orb, quarter, width), jnp.float32),
            pltpu.VMEM((packed, LANES), jnp.float32),
            pltpu.VMEM((groups, chunk, LANES), jnp.float32),
            pltpu.VMEM((chunk, LANES), jnp.float32),
            pltpu.VMEM((n_orb, chunk, LANES), jnp.float32),
            dma((n_orb,)), dma((n_orb,)),
            dma((groups,)), dma((groups,)),
            dma((n_orb,)), dma((n_orb,)),
            dma((groups,)), dma((groups,)),
        ],
        compiler_params=pltpu.CompilerParams(
            collective_id=1, has_side_effects=True, vmem_limit_bytes=40 * 2**20
        ),
        name="turn_and_gram",
    )(field, lower_list)
    if not inside:
        gram = lax.psum(gram, ("space", "orb"))
    return rows, gram


def invert_factor(matrix, inverse):
    size = matrix.shape[0]
    row_id = lax.broadcasted_iota(jnp.int32, (size, size), 0)
    column_id = lax.broadcasted_iota(jnp.int32, (size, size), 1)
    inverse[...] = jnp.where(row_id == column_id, 1.0, 0.0)
    for start in range(0, size, GROUP):
        below = start + GROUP
        rows = [matrix[start + b : start + b + 1, :] for b in range(GROUP)]
        eyes = [inverse[start + b : start + b + 1, :] for b in range(GROUP)]
        entry = {
            (b, c): jnp.broadcast_to(rows[b][:, start + c : start + c + 1], (1, size))
            for b in range(GROUP)
            for c in range(b + 1)
        }
        lower, scale, done = {}, [], []
        for b in range(GROUP):
            scale.append(lax.rsqrt(entry[b, b]))
            for i in range(b + 1, GROUP):
                lower[i, b] = entry[i, b] * scale[b]
            for i in range(b + 1, GROUP):
                for j in range(b + 1, i + 1):
                    entry[i, j] = entry[i, j] - lower[i, b] * lower[j, b]
            done.append((rows[b] * scale[b], eyes[b] * scale[b]))
            for i in range(b + 1, GROUP):
                rows[i] = rows[i] - lower[i, b] * done[b][0]
                eyes[i] = eyes[i] - lower[i, b] * done[b][1]
        for b in range(GROUP):
            inverse[start + b : start + b + 1, :] = done[b][1]
        if below == size:
            break
        back = list(done)
        for b in reversed(range(GROUP)):
            back[b] = (back[b][0] * scale[b], back[b][1] * scale[b])
            for i in range(b):
                back[i] = (back[i][0] - lower[b, i] * back[b][0], back[i][1] - lower[b, i] * back[b][1])
        rest = matrix[below:, :]
        rest_eye = inverse[below:, :]
        raw = [jnp.broadcast_to(rest[:, start + c : start + c + 1], rest.shape) for c in range(GROUP)]
        for c in range(GROUP):
            rest = rest - raw[c] * back[c][0]
            rest_eye = rest_eye - raw[c] * back[c][1]
        matrix[below:, :] = rest
        inverse[below:, :] = rest_eye


def rotate_kernel(rows, gram, rotated, lower, block, inverse):
    columns = rows.shape[1]
    blocks = columns // LANES
    lower[...] = jnp.zeros_like(lower)
    rotated[...] = jnp.zeros_like(rotated)
    last, second = ((1,), (1,)), ((1,), (1,))

    def one_block(k, carry):
        here = pl.ds(pl.multiple_of(k * LANES, LANES), LANES)
        spot = (k * (k + 3)) // 2
        own = lower[k]
        diagonal = gram[pl.ds(pl.multiple_of(spot * LANES, LANES), LANES), :]
        block[...] = diagonal - exact_dot(own, own, last)
        invert_factor(block, inverse)
        for i in range(1, blocks):

            @pl.when(i > k)
            def _():
                at = (i * (i + 1)) // 2 + k
                under = gram[pl.ds(pl.multiple_of(at * LANES, LANES), LANES), :]
                under = under - exact_dot(lower[i], own, last)
                lower[i, :, here] = exact_dot(under, inverse[...], second)

        left = rows[:, here] - exact_dot(rotated[...], own, last)
        rotated[:, here] = exact_dot(left, inverse[...], second)
        return carry

    lax.fori_loop(0, blocks, one_block, 0)


def rotate(rows, gram):
    columns = rows.shape[1]
    vmem = pl.BlockSpec(memory_space=pltpu.VMEM)
    return pl.pallas_call(
        rotate_kernel,
        out_shape=jax.ShapeDtypeStruct(rows.shape, jnp.float32),
        in_specs=[vmem, vmem],
        out_specs=vmem,
        scratch_shapes=[
            pltpu.VMEM((columns // LANES, LANES, columns), jnp.float32),
            pltpu.VMEM((LANES, LANES), jnp.float32),
            pltpu.VMEM((LANES, LANES), jnp.float32),
        ],
        compiler_params=pltpu.CompilerParams(vmem_limit_bytes=40 * 2**20),
        name="rotate",
    )(rows, gram)


def shards(wavefunctions, cell_ham, cell_nodes, cell_count, upper_nodes, lower_nodes):
    n_space, n_orb = lax.axis_size("space"), lax.axis_size("orb")
    current = filtered_block(
        wavefunctions[0], cell_ham[0], cell_nodes[0], cell_count[0], upper_nodes[0], lower_nodes[0], n_space
    )
    rows, gram = turn_and_gram(current, lower_nodes, n_space, n_orb)
    return rotate(rows, gram)[None]


def solution(mesh):
    in_specs = (
        P("space", None, "orb"),
        P("space", None, None, None),
        P("space", None, None),
        P("space"),
        P("space", None),
        P("space", None),
    )
    out_specs = P("space", "orb", None)
    return jax.shard_map(shards, mesh=mesh, in_specs=in_specs, out_specs=out_specs, check_vma=False)
```

```python
import functools

import jax
import jax.numpy as jnp
from jax import lax
from jax.experimental import pallas as pl
from jax.experimental.pallas import tpu as pltpu
from jax.sharding import PartitionSpec as P

DEGREE = 3
LANES = 128
GROUP = 8
MESH = pl.DeviceIdType.MESH


center_shift = 0.5
half_width = 2.0


def split(values):
    high = values.astype(jnp.bfloat16)
    return high, (values - high.astype(jnp.float32)).astype(jnp.bfloat16)


def plain_dot(left, right):
    return lax.dot_general(left, right, (((1,), (0,)), ((), ())), preferred_element_type=jnp.float32)


def folded(product):
    return product[:, :LANES] + product[:, LANES:]


def dense_rows(count, width):
    return count * width // LANES if 4 * width == 3 * LANES and count % 32 == 0 else count


def dense(values, width):
    count = values.shape[0]
    if dense_rows(count, width) == count:
        return values
    rest, side = count // 4, LANES - width
    tail = values[count - rest :, :]
    beside = [tail[:, at : at + side] for at in range(0, width, side)]
    return jnp.concatenate([values[: count - rest, :width], jnp.concatenate(beside, axis=0)], axis=1)


def sparse(values, count, width):
    if dense_rows(count, width) == count:
        return values[:, :width]
    rest = count // 4
    beside = [values[at : at + rest, width:] for at in range(0, count - rest, rest)]
    return jnp.concatenate([values[:, :width], jnp.concatenate(beside, axis=1)], axis=0)


def widened(values):
    room = LANES - values.shape[1]
    return jnp.concatenate([values, jnp.zeros((values.shape[0], room), values.dtype)], axis=1) if room else values


def filter_kernel(n_space, n_orb, degree, start, matrices, node_row, list_row, out, gather, scatter, pick, place, stack, raw,
                  fields, packed, cell_out, sums, outgoing, arriving, load_sem, send_sem, recv_sem):
    space = lax.axis_index("space")
    nodes, width = start.shape
    cells, doubled, cell_size = stack.shape
    slots = list_row.shape[1] // 2
    has_above, has_below = space < n_space - 1, space > 0

    def load(cell):
        return pltpu.make_async_copy(matrices.at[cell], raw.at[cell % 2], load_sem.at[cell])

    for cell in range(min(cells, 2)):
        load(cell).start()
    arriving[...] = jnp.zeros_like(arriving)

    barrier = pltpu.get_barrier_semaphore()

    @pl.when(has_above)
    def _():
        pl.semaphore_signal(barrier, inc=1, device_id={"space": space + 1}, device_id_type=MESH)

    @pl.when(has_below)
    def _():
        pl.semaphore_signal(barrier, inc=1, device_id={"space": space - 1}, device_id_type=MESH)

    lane = lax.broadcasted_iota(jnp.int32, (LANES, LANES), 1).astype(jnp.float32)
    sublane = lax.broadcasted_iota(jnp.int32, (LANES, LANES), 0).astype(jnp.float32)

    def ones_where(condition):
        return jnp.where(condition, 1.0, 0.0).astype(jnp.bfloat16)

    def tile_at(index):
        return pl.ds(pl.multiple_of(index * LANES, LANES), LANES)

    def upright(row):
        return jnp.transpose(jnp.broadcast_to(row, (LANES, LANES)))

    def gather_rows(chunk, carry):
        here = tile_at(chunk)
        column = upright(node_row[:, here])
        for tile in range(nodes // LANES):
            gather[here, tile * LANES : (tile + 1) * LANES] = ones_where(column == lane + float(tile * LANES))
        return carry

    def pick_rows(chunk, carry):
        here = tile_at(chunk)
        column = upright(list_row[:, here])
        for tile in range(node_row.shape[1] // LANES):
            there = slice(tile * LANES, (tile + 1) * LANES)
            pick[here, there] = ones_where(column == node_row[:, there])
        return carry

    def node_rows(chunk, carry):
        here = tile_at(chunk)
        node = sublane + (chunk * LANES).astype(jnp.float32)
        for tile in range(node_row.shape[1] // LANES):
            there = slice(tile * LANES, (tile + 1) * LANES)
            scatter[here, there] = ones_where(node == node_row[:, there])
        for tile in range(2 * slots // LANES):
            there = slice(tile * LANES, (tile + 1) * LANES)
            other = (tile * LANES + slots) % (2 * slots)
            place[here, there] = ones_where(node == list_row[:, other : other + LANES])
        values = widened(start[here, :])
        fields[0, here, :] = values
        fields[1, here, :] = values
        high, low = split(values)
        packed[here, :LANES] = high
        packed[here, LANES:] = low
        return carry

    lax.fori_loop(0, node_row.shape[1] // LANES, gather_rows, 0)
    for cell in range(cells):
        load(cell).wait()

        def split_rows(chunk, carry):
            here = tile_at(chunk)
            high, low = split(raw[cell % 2, here, :])
            stack[cell, here, :] = high
            stack[cell, pl.ds(pl.multiple_of(cell_size + chunk * LANES, LANES), LANES), :] = low
            return carry

        lax.fori_loop(0, cell_size // LANES, split_rows, 0)
        if cell + 2 < cells:
            load(cell + 2).start()
        if cell == 0:
            lax.fori_loop(0, 2 * slots // LANES, pick_rows, 0)
        if cell == min(cells - 1, 1):
            lax.fori_loop(0, nodes // LANES, node_rows, 0)
    pl.semaphore_wait(barrier, has_above.astype(jnp.int32) + has_below.astype(jnp.int32))

    part = nodes // 3 if nodes % (3 * LANES) == 0 else LANES

    def apply(step, carry):
        def one_cell(cell, carry):
            here = pl.ds(pl.multiple_of(cell * cell_size, LANES), cell_size)
            local = plain_dot(gather[here, :], packed[...]).astype(jnp.bfloat16)
            high_part = plain_dot(stack[cell, :cell_size, :], local)
            low_part = plain_dot(stack[cell, cell_size:, :], local[:, :LANES])
            high, low = split(folded(high_part) + low_part)
            cell_out[here, :LANES] = high
            cell_out[here, LANES:] = low
            return carry

        lax.fori_loop(0, cells, one_cell, 0)

        def transfer(way, towards):
            return pltpu.make_async_remote_copy(
                src_ref=outgoing.at[way],
                dst_ref=arriving.at[step, way],
                send_sem=send_sem.at[step, way],
                recv_sem=recv_sem.at[step, way],
                device_id={"space": towards},
                device_id_type=MESH,
            )

        down, up = transfer(0, space - 1), transfer(1, space + 1)
        outgoing[0] = dense(folded(plain_dot(pick[:slots, :], cell_out[...])), width)

        @pl.when(has_below)
        def _():
            down.start()

        outgoing[1] = dense(folded(plain_dot(pick[slots:, :], cell_out[...])), width)

        @pl.when(has_above)
        def _():
            up.start()

        def node_sums(chunk, carry):
            here = pl.ds(pl.multiple_of(chunk * part, LANES), part)
            sums[here, :] = folded(plain_dot(scatter[here, :], cell_out[...]))
            return carry

        lax.fori_loop(0, nodes // part, node_sums, 0)

        @pl.when(has_below)
        def _():
            down.wait_send()
            up.wait_recv()

        @pl.when(has_above)
        def _():
            up.wait_send()
            down.wait_recv()

        new, old = lax.rem(step + 1, 2), lax.rem(step, 2)
        first = step == 0
        scale = jnp.where(first, 1.0 / half_width, 2.0 / half_width)
        keep = jnp.where(first, 0.0, 1.0)
        parts = [split(widened(sparse(arriving[step, way], slots, width))) for way in range(2)]
        arrived = jnp.concatenate([jnp.concatenate(pair, axis=1) for pair in parts], axis=0)

        def advance(chunk, carry):
            here = pl.ds(pl.multiple_of(chunk * part, LANES), part)
            total = sums[here, :] + folded(plain_dot(place[here, :], arrived))
            value = scale * (total - center_shift * fields[old, here, :]) - keep * fields[new, here, :]
            fields[new, here, :] = value
            high, low = split(value)
            packed[here, :LANES] = high
            packed[here, LANES:] = low
            return carry

        lax.fori_loop(0, nodes // part, advance, 0)
        return carry

    lax.fori_loop(0, degree, apply, 0)
    quarter = nodes // n_orb
    for which in range(n_orb):
        out[which] = dense(fields[degree % 2, which * quarter : (which + 1) * quarter, :width], width)


def filtered_block(start, matrices, node_map, live_cells, upper_list, lower_list, n_space, n_orb):
    nodes, width = start.shape
    cells, cell_nodes = node_map.shape
    cell_size = -(-cell_nodes // LANES) * LANES
    room = cell_size - cell_nodes
    slots = upper_list.shape[0]

    padded = jnp.pad(matrices, ((0, 0), (0, room), (0, room)))
    live = jnp.arange(cells)[:, None] < live_cells
    node_row = jnp.pad(jnp.where(live, node_map, -1), ((0, 0), (0, room)), constant_values=-1)
    node_row = node_row.reshape(1, cells * cell_size).astype(jnp.float32)
    list_row = jnp.concatenate([lower_list, upper_list]).reshape(1, 2 * slots).astype(jnp.float32)

    sent = dense_rows(nodes // n_orb, width)
    packed_width = LANES if sent != nodes // n_orb else width
    slot_rows = dense_rows(slots, width)
    vmem, anywhere = pl.BlockSpec(memory_space=pltpu.VMEM), pl.BlockSpec(memory_space=pl.ANY)
    dma = pltpu.SemaphoreType.DMA
    every, half = jnp.float32, jnp.bfloat16
    return pl.pallas_call(
        functools.partial(filter_kernel, n_space, n_orb, DEGREE),
        out_shape=jax.ShapeDtypeStruct((n_orb, sent, packed_width), jnp.float32),
        in_specs=[vmem, anywhere, vmem, vmem],
        out_specs=vmem,
        scratch_shapes=[
            pltpu.VMEM((cells * cell_size, nodes), half),
            pltpu.VMEM((nodes, cells * cell_size), half),
            pltpu.VMEM((2 * slots, cells * cell_size), half),
            pltpu.VMEM((nodes, 2 * slots), half),
            pltpu.VMEM((cells, 2 * cell_size, cell_size), half),
            pltpu.VMEM((2, cell_size, cell_size), every),
            pltpu.VMEM((2, nodes, LANES), every),
            pltpu.VMEM((nodes, 2 * LANES), half),
            pltpu.VMEM((cells * cell_size, 2 * LANES), half),
            pltpu.VMEM((nodes, LANES), every),
            pltpu.VMEM((2, slot_rows, LANES), every),
            pltpu.VMEM((DEGREE, 2, slot_rows, LANES), every),
            dma((cells,)),
            dma((DEGREE, 2)),
            dma((DEGREE, 2)),
        ],
        compiler_params=pltpu.CompilerParams(
            collective_id=2, has_side_effects=True, vmem_limit_bytes=58 * 2**20
        ),
        name="filter",
    )(start, padded, node_row, list_row)


def exact_dot(left, right, dims):
    return lax.dot_general(
        left,
        right,
        (dims, ((), ())),
        precision=lax.Precision.HIGHEST,
        preferred_element_type=jnp.float32,
    )


def block_pairs(blocks):
    return [(i, j) for i in range(blocks) for j in range(i + 1)]


def gram_kernel(n_space, n_orb, node_total, inside, field, lower_list, rows_out, gram_out, pieces, local, parts, slab, others,
                turn_send, turn_recv, split_send, split_recv, orb_send, orb_recv, join_send, join_recv):
    space, orb = lax.axis_index("space"), lax.axis_index("orb")
    quarter, columns = rows_out.shape
    width = columns // n_orb
    partners = n_orb - 1

    barrier = pltpu.get_barrier_semaphore()
    for step in range(1, n_orb):
        pl.semaphore_signal(barrier, inc=1, device_id={"orb": lax.rem(orb + step, n_orb)}, device_id_type=MESH)
    if inside:
        partners += n_space - 1
        for step in range(1, n_space):
            pl.semaphore_signal(barrier, inc=1, device_id={"space": lax.rem(space + step, n_space)}, device_id_type=MESH)
    pl.semaphore_wait(barrier, partners)

    def exchange(axis, size, here, send_sems, recv_sems, source, target):
        copies = []
        for step in range(1, size):
            other = lax.rem(here + step, size)
            copy = pltpu.make_async_remote_copy(
                src_ref=source(other),
                dst_ref=target,
                send_sem=send_sems.at[step],
                recv_sem=recv_sems.at[step],
                device_id={axis: other},
                device_id_type=MESH,
            )
            copy.start()
            copies.append(copy)
        return copies

    copies = exchange("orb", n_orb, orb, turn_send, turn_recv, lambda other: field.at[other], pieces.at[orb])
    pieces[orb] = field[orb]
    node = lax.broadcasted_iota(jnp.int32, (quarter, lower_list.shape[1]), 0) + orb * quarter
    hits = jnp.where(node == lower_list[...], 1.0, 0.0)
    weight = (1.0 - jnp.max(hits, axis=1, keepdims=True)) * (1.0 / (n_space * node_total))
    for copy in copies:
        copy.wait()
    for which in range(n_orb):
        rows_out[:, which * width : (which + 1) * width] = sparse(pieces[which], quarter, width)

    blocks = columns // LANES
    for spot, (i, j) in enumerate(block_pairs(blocks)):
        left = rows_out[:, i * LANES : (i + 1) * LANES] * weight
        right = rows_out[:, j * LANES : (j + 1) * LANES]
        term = exact_dot(left, right, ((0,), (0,)))
        if inside:
            local[spot * LANES : (spot + 1) * LANES, :] = term
        else:
            gram_out[spot * LANES : (spot + 1) * LANES, :] = term
    if not inside:
        return

    chunk = local.shape[0] // n_space

    def chunk_of(which):
        return local.at[pl.ds(pl.multiple_of(which * chunk, 8), chunk)]

    copies = exchange("space", n_space, space, split_send, split_recv, chunk_of, parts.at[space])
    parts[space] = local[pl.ds(pl.multiple_of(space * chunk, 8), chunk), :]
    for copy in copies:
        copy.wait()
    slab[...] = jnp.sum(parts[...], axis=0)

    copies = exchange("orb", n_orb, orb, orb_send, orb_recv, lambda _: slab, others.at[orb])
    others[orb] = slab[...]
    for copy in copies:
        copy.wait()
    mine = pl.ds(pl.multiple_of(space * chunk, 8), chunk)
    gram_out[mine, :] = jnp.sum(others[...], axis=0)
    copies = exchange("space", n_space, space, join_send, join_recv, lambda _: gram_out.at[mine], gram_out.at[mine])
    for copy in copies:
        copy.wait()


def turn_and_gram(field, lower_list, node_total, width, n_space, n_orb):
    quarter, columns = node_total // n_orb, width * n_orb
    packed = len(block_pairs(columns // LANES)) * LANES
    inside = n_space <= 8 and packed % (8 * n_space) == 0
    groups = n_space if inside else 1
    chunk = packed // groups
    dma = pltpu.SemaphoreType.DMA
    vmem = pl.BlockSpec(memory_space=pltpu.VMEM)
    rows, gram = pl.pallas_call(
        functools.partial(gram_kernel, n_space, n_orb, node_total, inside),
        out_shape=(
            jax.ShapeDtypeStruct((quarter, columns), jnp.float32),
            jax.ShapeDtypeStruct((packed, LANES), jnp.float32),
        ),
        in_specs=[vmem, vmem],
        out_specs=(vmem, vmem),
        scratch_shapes=[
            pltpu.VMEM(field.shape, jnp.float32),
            pltpu.VMEM((packed, LANES), jnp.float32),
            pltpu.VMEM((groups, chunk, LANES), jnp.float32),
            pltpu.VMEM((chunk, LANES), jnp.float32),
            pltpu.VMEM((n_orb, chunk, LANES), jnp.float32),
            dma((n_orb,)), dma((n_orb,)),
            dma((groups,)), dma((groups,)),
            dma((n_orb,)), dma((n_orb,)),
            dma((groups,)), dma((groups,)),
        ],
        compiler_params=pltpu.CompilerParams(
            collective_id=1, has_side_effects=True, vmem_limit_bytes=40 * 2**20
        ),
        name="turn_and_gram",
    )(field, lower_list)
    if not inside:
        gram = lax.psum(gram, ("space", "orb"))
    return rows, gram


def invert_factor(matrix, inverse):
    size = matrix.shape[0]
    row_id = lax.broadcasted_iota(jnp.int32, (size, size), 0)
    column_id = lax.broadcasted_iota(jnp.int32, (size, size), 1)
    inverse[...] = jnp.where(row_id == column_id, 1.0, 0.0)
    for start in range(0, size, GROUP):
        below = start + GROUP
        rows = [matrix[start + b : start + b + 1, :] for b in range(GROUP)]
        eyes = [inverse[start + b : start + b + 1, :] for b in range(GROUP)]
        entry = {
            (b, c): jnp.broadcast_to(rows[b][:, start + c : start + c + 1], (1, size))
            for b in range(GROUP)
            for c in range(b + 1)
        }
        lower, scale, done = {}, [], []
        for b in range(GROUP):
            scale.append(lax.rsqrt(entry[b, b]))
            for i in range(b + 1, GROUP):
                lower[i, b] = entry[i, b] * scale[b]
            for i in range(b + 1, GROUP):
                for j in range(b + 1, i + 1):
                    entry[i, j] = entry[i, j] - lower[i, b] * lower[j, b]
            done.append((rows[b] * scale[b], eyes[b] * scale[b]))
            for i in range(b + 1, GROUP):
                rows[i] = rows[i] - lower[i, b] * done[b][0]
                eyes[i] = eyes[i] - lower[i, b] * done[b][1]
        for b in range(GROUP):
            inverse[start + b : start + b + 1, :] = done[b][1]
        if below == size:
            break
        back = list(done)
        for b in reversed(range(GROUP)):
            back[b] = (back[b][0] * scale[b], back[b][1] * scale[b])
            for i in range(b):
                back[i] = (back[i][0] - lower[b, i] * back[b][0], back[i][1] - lower[b, i] * back[b][1])
        rest = matrix[below:, :]
        rest_eye = inverse[below:, :]
        raw = [jnp.broadcast_to(rest[:, start + c : start + c + 1], rest.shape) for c in range(GROUP)]
        for c in range(GROUP):
            rest = rest - raw[c] * back[c][0]
            rest_eye = rest_eye - raw[c] * back[c][1]
        matrix[below:, :] = rest
        inverse[below:, :] = rest_eye


def rotate_kernel(rows, gram, rotated, lower, block, inverse):
    columns = rows.shape[1]
    blocks = columns // LANES
    lower[...] = jnp.zeros_like(lower)
    rotated[...] = jnp.zeros_like(rotated)
    last, second = ((1,), (1,)), ((1,), (1,))

    def one_block(k, carry):
        here = pl.ds(pl.multiple_of(k * LANES, LANES), LANES)
        spot = (k * (k + 3)) // 2
        own = lower[k]
        diagonal = gram[pl.ds(pl.multiple_of(spot * LANES, LANES), LANES), :]
        block[...] = diagonal - exact_dot(own, own, last)
        invert_factor(block, inverse)
        for i in range(1, blocks):

            @pl.when(i > k)
            def _():
                at = (i * (i + 1)) // 2 + k
                under = gram[pl.ds(pl.multiple_of(at * LANES, LANES), LANES), :]
                under = under - exact_dot(lower[i], own, last)
                lower[i, :, here] = exact_dot(under, inverse[...], second)

        left = rows[:, here] - exact_dot(rotated[...], own, last)
        rotated[:, here] = exact_dot(left, inverse[...], second)
        return carry

    lax.fori_loop(0, blocks, one_block, 0)


def rotate(rows, gram):
    columns = rows.shape[1]
    vmem = pl.BlockSpec(memory_space=pltpu.VMEM)
    return pl.pallas_call(
        rotate_kernel,
        out_shape=jax.ShapeDtypeStruct(rows.shape, jnp.float32),
        in_specs=[vmem, vmem],
        out_specs=vmem,
        scratch_shapes=[
            pltpu.VMEM((columns // LANES, LANES, columns), jnp.float32),
            pltpu.VMEM((LANES, LANES), jnp.float32),
            pltpu.VMEM((LANES, LANES), jnp.float32),
        ],
        compiler_params=pltpu.CompilerParams(vmem_limit_bytes=40 * 2**20),
        name="rotate",
    )(rows, gram)


def shards(wavefunctions, cell_ham, cell_nodes, cell_count, upper_nodes, lower_nodes):
    n_space, n_orb = lax.axis_size("space"), lax.axis_size("orb")
    current = filtered_block(
        wavefunctions[0], cell_ham[0], cell_nodes[0], cell_count[0], upper_nodes[0], lower_nodes[0],
        n_space, n_orb,
    )
    rows, gram = turn_and_gram(current, lower_nodes, *wavefunctions.shape[1:], n_space, n_orb)
    return rotate(rows, gram)[None]


def solution(mesh):
    in_specs = (
        P("space", None, "orb"),
        P("space", None, None, None),
        P("space", None, None),
        P("space"),
        P("space", None),
        P("space", None),
    )
    out_specs = P("space", "orb", None)
    return jax.shard_map(shards, mesh=mesh, in_specs=in_specs, out_specs=out_specs, check_vma=False)
```

```python
import functools

import jax
import jax.numpy as jnp
from jax import lax
from jax.experimental import pallas as pl
from jax.experimental.pallas import tpu as pltpu
from jax.sharding import PartitionSpec as P

DEGREE = 3
LANES = 128
GROUP = 8
MESH = pl.DeviceIdType.MESH


center_shift = 0.5
half_width = 2.0


def split(values):
    high = values.astype(jnp.bfloat16)
    return high, (values - high.astype(jnp.float32)).astype(jnp.bfloat16)


def plain_dot(left, right):
    return lax.dot_general(left, right, (((1,), (0,)), ((), ())), preferred_element_type=jnp.float32)


def folded(product):
    return product[:, :LANES] + product[:, LANES:]


def dense_rows(count, width):
    return count * width // LANES if 4 * width == 3 * LANES and count % 32 == 0 else count


def dense(values, width):
    count = values.shape[0]
    if dense_rows(count, width) == count:
        return values
    rest, side = count // 4, LANES - width
    tail = values[count - rest :, :]
    beside = [tail[:, at : at + side] for at in range(0, width, side)]
    return jnp.concatenate([values[: count - rest, :width], jnp.concatenate(beside, axis=0)], axis=1)


def sparse(values, count, width):
    if dense_rows(count, width) == count:
        return values[:, :width]
    rest = count // 4
    beside = [values[at : at + rest, width:] for at in range(0, count - rest, rest)]
    return jnp.concatenate([values[:, :width], jnp.concatenate(beside, axis=1)], axis=0)


def widened(values):
    room = LANES - values.shape[1]
    return jnp.concatenate([values, jnp.zeros((values.shape[0], room), values.dtype)], axis=1) if room else values


def filter_kernel(n_space, n_orb, degree, start, matrices, node_row, list_row, out, gather, scatter, pick, place, stack, raw,
                  fields, packed, cell_out, sums, outgoing, arriving, load_sem, send_sem, recv_sem):
    space = lax.axis_index("space")
    width, nodes = start.shape
    cells, doubled, cell_size = stack.shape
    cell_nodes = raw.shape[1]
    whole = cell_nodes // 8 * 8
    tail_at = whole // 16 * 16
    slots = list_row.shape[1] // 2
    has_above, has_below = space < n_space - 1, space > 0

    def load(cell):
        return pltpu.make_async_copy(matrices.at[cell], raw.at[cell % 2], load_sem.at[cell])

    for cell in range(min(cells, 2)):
        load(cell).start()
    arriving[...] = jnp.zeros_like(arriving)

    barrier = pltpu.get_barrier_semaphore()

    @pl.when(has_above)
    def _():
        pl.semaphore_signal(barrier, inc=1, device_id={"space": space + 1}, device_id_type=MESH)

    @pl.when(has_below)
    def _():
        pl.semaphore_signal(barrier, inc=1, device_id={"space": space - 1}, device_id_type=MESH)

    lane = lax.broadcasted_iota(jnp.int32, (LANES, LANES), 1).astype(jnp.float32)
    sublane = lax.broadcasted_iota(jnp.int32, (LANES, LANES), 0).astype(jnp.float32)

    def ones_where(condition):
        return jnp.where(condition, 1.0, 0.0).astype(jnp.bfloat16)

    def tile_at(index):
        return pl.ds(pl.multiple_of(index * LANES, LANES), LANES)

    def upright(row):
        return jnp.transpose(jnp.broadcast_to(row, (LANES, LANES)))

    def gather_rows(chunk, carry):
        here = tile_at(chunk)
        column = upright(node_row[:, here])
        for tile in range(nodes // LANES):
            gather[here, tile * LANES : (tile + 1) * LANES] = ones_where(column == lane + float(tile * LANES))
        return carry

    def pick_rows(chunk, carry):
        here = tile_at(chunk)
        column = upright(list_row[:, here])
        for tile in range(node_row.shape[1] // LANES):
            there = slice(tile * LANES, (tile + 1) * LANES)
            pick[here, there] = ones_where(column == node_row[:, there])
        return carry

    def node_rows(chunk, carry):
        here = tile_at(chunk)
        node = sublane + (chunk * LANES).astype(jnp.float32)
        for tile in range(node_row.shape[1] // LANES):
            there = slice(tile * LANES, (tile + 1) * LANES)
            scatter[here, there] = ones_where(node == node_row[:, there])
        for tile in range(2 * slots // LANES):
            there = slice(tile * LANES, (tile + 1) * LANES)
            other = (tile * LANES + slots) % (2 * slots)
            place[here, there] = ones_where(node == list_row[:, other : other + LANES])
        block = start[:, here]
        if width < LANES:
            block = jnp.concatenate([block, jnp.zeros((LANES - width, LANES), jnp.float32)], axis=0)
        values = jnp.transpose(block)
        fields[0, here, :] = values
        fields[1, here, :] = values
        high, low = split(values)
        packed[here, :LANES] = high
        packed[here, LANES:] = low
        return carry

    lax.fori_loop(0, node_row.shape[1] // LANES, gather_rows, 0)
    for cell in range(cells):
        load(cell).wait()

        def put_split(at, values):
            high, low = split(values)
            stack[cell, pl.ds(at, values.shape[0]), :] = high
            stack[cell, pl.ds(cell_size + at, values.shape[0]), :] = low

        def widen(values):
            room = cell_size - cell_nodes
            return jnp.concatenate([values, jnp.zeros((values.shape[0], room), jnp.float32)], axis=1)

        def split_rows(chunk, carry):
            put_split(pl.multiple_of(chunk * LANES, LANES), widen(raw[cell % 2, tile_at(chunk), :]))
            return carry

        lax.fori_loop(0, tail_at // LANES, split_rows, 0)
        done = tail_at // LANES * LANES
        if tail_at > done:
            put_split(done, widen(raw[cell % 2, done:tail_at, :]))
        if cell_size > tail_at:
            pieces = [widen(raw[cell % 2, tail_at:whole, :])] if whole > tail_at else []
            if cell_nodes > whole:
                row_id = lax.broadcasted_iota(jnp.int32, (8, cell_size), 0)
                block = jnp.zeros((8, cell_size), jnp.float32)
                for row in range(whole, cell_nodes):
                    value = jnp.broadcast_to(widen(raw[cell % 2, row : row + 1, :]), (8, cell_size))
                    block = jnp.where(row_id == row - whole, value, block)
                pieces.append(block)
            room = cell_size - tail_at - sum(piece.shape[0] for piece in pieces)
            if room:
                pieces.append(jnp.zeros((room, cell_size), jnp.float32))
            put_split(tail_at, jnp.concatenate(pieces, axis=0))
        if cell + 2 < cells:
            load(cell + 2).start()
        if cell == 0:
            lax.fori_loop(0, 2 * slots // LANES, pick_rows, 0)
        if cell == min(cells - 1, 1):
            lax.fori_loop(0, nodes // LANES, node_rows, 0)
    pl.semaphore_wait(barrier, has_above.astype(jnp.int32) + has_below.astype(jnp.int32))

    part = nodes // 3 if nodes % (3 * LANES) == 0 else LANES

    def apply(step, carry):
        def one_cell(cell, carry):
            here = pl.ds(pl.multiple_of(cell * cell_size, LANES), cell_size)
            local = plain_dot(gather[here, :], packed[...]).astype(jnp.bfloat16)
            high_part = plain_dot(stack[cell, :cell_size, :], local)
            low_part = plain_dot(stack[cell, cell_size:, :], local[:, :LANES])
            high, low = split(folded(high_part) + low_part)
            cell_out[here, :LANES] = high
            cell_out[here, LANES:] = low
            return carry

        lax.fori_loop(0, cells, one_cell, 0)

        def transfer(way, towards):
            return pltpu.make_async_remote_copy(
                src_ref=outgoing.at[way],
                dst_ref=arriving.at[step, way],
                send_sem=send_sem.at[step, way],
                recv_sem=recv_sem.at[step, way],
                device_id={"space": towards},
                device_id_type=MESH,
            )

        down, up = transfer(0, space - 1), transfer(1, space + 1)
        outgoing[0] = dense(folded(plain_dot(pick[:slots, :], cell_out[...])), width)

        @pl.when(has_below)
        def _():
            down.start()

        outgoing[1] = dense(folded(plain_dot(pick[slots:, :], cell_out[...])), width)

        @pl.when(has_above)
        def _():
            up.start()

        def node_sums(chunk, carry):
            here = pl.ds(pl.multiple_of(chunk * part, LANES), part)
            sums[here, :] = folded(plain_dot(scatter[here, :], cell_out[...]))
            return carry

        lax.fori_loop(0, nodes // part, node_sums, 0)

        @pl.when(has_below)
        def _():
            down.wait_send()
            up.wait_recv()

        @pl.when(has_above)
        def _():
            up.wait_send()
            down.wait_recv()

        new, old = lax.rem(step + 1, 2), lax.rem(step, 2)
        first = step == 0
        scale = jnp.where(first, 1.0 / half_width, 2.0 / half_width)
        keep = jnp.where(first, 0.0, 1.0)
        parts = [split(widened(sparse(arriving[step, way], slots, width))) for way in range(2)]
        arrived = jnp.concatenate([jnp.concatenate(pair, axis=1) for pair in parts], axis=0)

        def advance(chunk, carry):
            here = pl.ds(pl.multiple_of(chunk * part, LANES), part)
            total = sums[here, :] + folded(plain_dot(place[here, :], arrived))
            value = scale * (total - center_shift * fields[old, here, :]) - keep * fields[new, here, :]
            fields[new, here, :] = value
            high, low = split(value)
            packed[here, :LANES] = high
            packed[here, LANES:] = low
            return carry

        lax.fori_loop(0, nodes // part, advance, 0)
        return carry

    lax.fori_loop(0, degree, apply, 0)
    quarter = nodes // n_orb
    for which in range(n_orb):
        out[which] = dense(fields[degree % 2, which * quarter : (which + 1) * quarter, :width], width)


def filtered_block(start, matrices, node_map, live_cells, upper_list, lower_list, n_space, n_orb):
    nodes, width = start.shape
    cells, cell_nodes = node_map.shape
    cell_size = -(-cell_nodes // LANES) * LANES
    room = cell_size - cell_nodes
    slots = upper_list.shape[0]

    live = jnp.arange(cells)[:, None] < live_cells
    node_row = jnp.pad(jnp.where(live, node_map, -1), ((0, 0), (0, room)), constant_values=-1)
    node_row = node_row.reshape(1, cells * cell_size).astype(jnp.float32)
    list_row = jnp.concatenate([lower_list, upper_list]).reshape(1, 2 * slots).astype(jnp.float32)

    sent = dense_rows(nodes // n_orb, width)
    packed_width = LANES if sent != nodes // n_orb else width
    slot_rows = dense_rows(slots, width)
    vmem, anywhere = pl.BlockSpec(memory_space=pltpu.VMEM), pl.BlockSpec(memory_space=pl.ANY)
    dma = pltpu.SemaphoreType.DMA
    every, half = jnp.float32, jnp.bfloat16
    return pl.pallas_call(
        functools.partial(filter_kernel, n_space, n_orb, DEGREE),
        out_shape=jax.ShapeDtypeStruct((n_orb, sent, packed_width), jnp.float32),
        in_specs=[vmem, anywhere, vmem, vmem],
        out_specs=vmem,
        scratch_shapes=[
            pltpu.VMEM((cells * cell_size, nodes), half),
            pltpu.VMEM((nodes, cells * cell_size), half),
            pltpu.VMEM((2 * slots, cells * cell_size), half),
            pltpu.VMEM((nodes, 2 * slots), half),
            pltpu.VMEM((cells, 2 * cell_size, cell_size), half),
            pltpu.VMEM((2, cell_nodes, cell_nodes), every),
            pltpu.VMEM((2, nodes, LANES), every),
            pltpu.VMEM((nodes, 2 * LANES), half),
            pltpu.VMEM((cells * cell_size, 2 * LANES), half),
            pltpu.VMEM((nodes, LANES), every),
            pltpu.VMEM((2, slot_rows, LANES), every),
            pltpu.VMEM((DEGREE, 2, slot_rows, LANES), every),
            dma((cells,)),
            dma((DEGREE, 2)),
            dma((DEGREE, 2)),
        ],
        compiler_params=pltpu.CompilerParams(
            collective_id=2, has_side_effects=True, vmem_limit_bytes=58 * 2**20
        ),
        name="filter",
    )(jnp.swapaxes(start, 0, 1), matrices, node_row, list_row)


def exact_dot(left, right, dims):
    return lax.dot_general(
        left,
        right,
        (dims, ((), ())),
        precision=lax.Precision.HIGHEST,
        preferred_element_type=jnp.float32,
    )


def block_pairs(blocks):
    return [(i, j) for i in range(blocks) for j in range(i + 1)]


def gram_kernel(n_space, n_orb, node_total, inside, field, lower_list, rows_out, gram_out, pieces, local, parts, slab, others,
                turn_send, turn_recv, split_send, split_recv, orb_send, orb_recv, join_send, join_recv):
    space, orb = lax.axis_index("space"), lax.axis_index("orb")
    quarter, columns = rows_out.shape
    width = columns // n_orb
    partners = n_orb - 1

    barrier = pltpu.get_barrier_semaphore()
    for step in range(1, n_orb):
        pl.semaphore_signal(barrier, inc=1, device_id={"orb": lax.rem(orb + step, n_orb)}, device_id_type=MESH)
    if inside:
        partners += n_space - 1
        for step in range(1, n_space):
            pl.semaphore_signal(barrier, inc=1, device_id={"space": lax.rem(space + step, n_space)}, device_id_type=MESH)
    pl.semaphore_wait(barrier, partners)

    def exchange(axis, size, here, send_sems, recv_sems, source, target):
        copies = []
        for step in range(1, size):
            other = lax.rem(here + step, size)
            copy = pltpu.make_async_remote_copy(
                src_ref=source(other),
                dst_ref=target,
                send_sem=send_sems.at[step],
                recv_sem=recv_sems.at[step],
                device_id={axis: other},
                device_id_type=MESH,
            )
            copy.start()
            copies.append(copy)
        return copies

    copies = exchange("orb", n_orb, orb, turn_send, turn_recv, lambda other: field.at[other], pieces.at[orb])
    pieces[orb] = field[orb]
    node = lax.broadcasted_iota(jnp.int32, (quarter, lower_list.shape[1]), 0) + orb * quarter
    hits = jnp.where(node == lower_list[...], 1.0, 0.0)
    weight = (1.0 - jnp.max(hits, axis=1, keepdims=True)) * (1.0 / (n_space * node_total))
    for copy in copies:
        copy.wait()
    for which in range(n_orb):
        rows_out[:, which * width : (which + 1) * width] = sparse(pieces[which], quarter, width)

    blocks = columns // LANES
    for spot, (i, j) in enumerate(block_pairs(blocks)):
        left = rows_out[:, i * LANES : (i + 1) * LANES] * weight
        right = rows_out[:, j * LANES : (j + 1) * LANES]
        term = exact_dot(left, right, ((0,), (0,)))
        if inside:
            local[spot * LANES : (spot + 1) * LANES, :] = term
        else:
            gram_out[spot * LANES : (spot + 1) * LANES, :] = term
    if not inside:
        return

    chunk = local.shape[0] // n_space

    def chunk_of(which):
        return local.at[pl.ds(pl.multiple_of(which * chunk, 8), chunk)]

    copies = exchange("space", n_space, space, split_send, split_recv, chunk_of, parts.at[space])
    parts[space] = local[pl.ds(pl.multiple_of(space * chunk, 8), chunk), :]
    for copy in copies:
        copy.wait()
    slab[...] = jnp.sum(parts[...], axis=0)

    copies = exchange("orb", n_orb, orb, orb_send, orb_recv, lambda _: slab, others.at[orb])
    others[orb] = slab[...]
    for copy in copies:
        copy.wait()
    mine = pl.ds(pl.multiple_of(space * chunk, 8), chunk)
    gram_out[mine, :] = jnp.sum(others[...], axis=0)
    copies = exchange("space", n_space, space, join_send, join_recv, lambda _: gram_out.at[mine], gram_out.at[mine])
    for copy in copies:
        copy.wait()


def turn_and_gram(field, lower_list, node_total, width, n_space, n_orb):
    quarter, columns = node_total // n_orb, width * n_orb
    packed = len(block_pairs(columns // LANES)) * LANES
    inside = n_space <= 8 and packed % (8 * n_space) == 0
    groups = n_space if inside else 1
    chunk = packed // groups
    dma = pltpu.SemaphoreType.DMA
    vmem = pl.BlockSpec(memory_space=pltpu.VMEM)
    rows, gram = pl.pallas_call(
        functools.partial(gram_kernel, n_space, n_orb, node_total, inside),
        out_shape=(
            jax.ShapeDtypeStruct((quarter, columns), jnp.float32),
            jax.ShapeDtypeStruct((packed, LANES), jnp.float32),
        ),
        in_specs=[vmem, vmem],
        out_specs=(vmem, vmem),
        scratch_shapes=[
            pltpu.VMEM(field.shape, jnp.float32),
            pltpu.VMEM((packed, LANES), jnp.float32),
            pltpu.VMEM((groups, chunk, LANES), jnp.float32),
            pltpu.VMEM((chunk, LANES), jnp.float32),
            pltpu.VMEM((n_orb, chunk, LANES), jnp.float32),
            dma((n_orb,)), dma((n_orb,)),
            dma((groups,)), dma((groups,)),
            dma((n_orb,)), dma((n_orb,)),
            dma((groups,)), dma((groups,)),
        ],
        compiler_params=pltpu.CompilerParams(
            collective_id=1, has_side_effects=True, vmem_limit_bytes=40 * 2**20
        ),
        name="turn_and_gram",
    )(field, lower_list)
    if not inside:
        gram = lax.psum(gram, ("space", "orb"))
    return rows, gram


def invert_factor(matrix, inverse):
    size = matrix.shape[0]
    row_id = lax.broadcasted_iota(jnp.int32, (size, size), 0)
    column_id = lax.broadcasted_iota(jnp.int32, (size, size), 1)
    inverse[...] = jnp.where(row_id == column_id, 1.0, 0.0)
    for start in range(0, size, GROUP):
        below = start + GROUP
        rows = [matrix[start + b : start + b + 1, :] for b in range(GROUP)]
        eyes = [inverse[start + b : start + b + 1, :] for b in range(GROUP)]
        entry = {
            (b, c): jnp.broadcast_to(rows[b][:, start + c : start + c + 1], (1, size))
            for b in range(GROUP)
            for c in range(b + 1)
        }
        lower, scale, done = {}, [], []
        for b in range(GROUP):
            scale.append(lax.rsqrt(entry[b, b]))
            for i in range(b + 1, GROUP):
                lower[i, b] = entry[i, b] * scale[b]
            for i in range(b + 1, GROUP):
                for j in range(b + 1, i + 1):
                    entry[i, j] = entry[i, j] - lower[i, b] * lower[j, b]
            done.append((rows[b] * scale[b], eyes[b] * scale[b]))
            for i in range(b + 1, GROUP):
                rows[i] = rows[i] - lower[i, b] * done[b][0]
                eyes[i] = eyes[i] - lower[i, b] * done[b][1]
        for b in range(GROUP):
            inverse[start + b : start + b + 1, :] = done[b][1]
        if below == size:
            break
        back = list(done)
        for b in reversed(range(GROUP)):
            back[b] = (back[b][0] * scale[b], back[b][1] * scale[b])
            for i in range(b):
                back[i] = (back[i][0] - lower[b, i] * back[b][0], back[i][1] - lower[b, i] * back[b][1])
        rest = matrix[below:, :]
        rest_eye = inverse[below:, :]
        raw = [jnp.broadcast_to(rest[:, start + c : start + c + 1], rest.shape) for c in range(GROUP)]
        for c in range(GROUP):
            rest = rest - raw[c] * back[c][0]
            rest_eye = rest_eye - raw[c] * back[c][1]
        matrix[below:, :] = rest
        inverse[below:, :] = rest_eye


def parts_dot(left, right):
    dims = (((1,), (1,)), ((), ()))
    (left_high, left_low), (right_high, right_low) = split(left), split(right)

    def product(a, b):
        return lax.dot_general(a, b, dims, preferred_element_type=jnp.float32)

    return product(left_high, right_high) + (product(left_high, right_low) + product(left_low, right_high))


def rotate_kernel(rows, gram, rotated, lower, block, inverse):
    blocks = rows.shape[1] // LANES
    last = ((1,), (1,))

    def span(k):
        return slice(k * LANES, (k + 1) * LANES)

    for k in range(blocks):
        before = slice(0, k * LANES)
        spot = k * (k + 3) // 2
        diagonal = gram[span(spot), :]
        if k:
            own = lower[k, :, before]
            diagonal = diagonal - exact_dot(own, own, last)
        block[k] = diagonal
        invert_factor(block.at[k], inverse.at[k])
        solved = inverse[k]
        for i in range(k + 1, blocks):
            under = gram[span(i * (i + 1) // 2 + k), :]
            if k:
                under = under - exact_dot(lower[i, :, before], own, last)
            lower[i, :, span(k)] = exact_dot(under, solved, last)
        left = rows[:, span(k)]
        if k:
            left = left - parts_dot(rotated[:, before], own)
        rotated[:, span(k)] = parts_dot(left, solved)


def rotate(rows, gram):
    columns = rows.shape[1]
    vmem = pl.BlockSpec(memory_space=pltpu.VMEM)
    return pl.pallas_call(
        rotate_kernel,
        out_shape=jax.ShapeDtypeStruct(rows.shape, jnp.float32),
        in_specs=[vmem, vmem],
        out_specs=vmem,
        scratch_shapes=[
            pltpu.VMEM((columns // LANES, LANES, columns), jnp.float32),
            pltpu.VMEM((columns // LANES, LANES, LANES), jnp.float32),
            pltpu.VMEM((columns // LANES, LANES, LANES), jnp.float32),
        ],
        compiler_params=pltpu.CompilerParams(vmem_limit_bytes=40 * 2**20),
        name="rotate",
    )(rows, gram)


def shards(wavefunctions, cell_ham, cell_nodes, cell_count, upper_nodes, lower_nodes):
    n_space, n_orb = lax.axis_size("space"), lax.axis_size("orb")
    current = filtered_block(
        wavefunctions[0], cell_ham[0], cell_nodes[0], cell_count[0], upper_nodes[0], lower_nodes[0],
        n_space, n_orb,
    )
    rows, gram = turn_and_gram(current, lower_nodes, *wavefunctions.shape[1:], n_space, n_orb)
    return rotate(rows, gram)[None]


def solution(mesh):
    in_specs = (
        P("space", None, "orb"),
        P("space", None, None, None),
        P("space", None, None),
        P("space"),
        P("space", None),
        P("space", None),
    )
    out_specs = P("space", "orb", None)
    return jax.shard_map(shards, mesh=mesh, in_specs=in_specs, out_specs=out_specs, check_vma=False)
```

```python
import functools

import jax
import jax.numpy as jnp
from jax import lax
from jax.experimental import pallas as pl
from jax.experimental.pallas import tpu as pltpu
from jax.sharding import PartitionSpec as P

DEGREE = 3
LANES = 128
GROUP = 8
MESH = pl.DeviceIdType.MESH


center_shift = 0.5
half_width = 2.0


def split(values):
    high = values.astype(jnp.bfloat16)
    return high, (values - high.astype(jnp.float32)).astype(jnp.bfloat16)


def plain_dot(left, right):
    return lax.dot_general(left, right, (((1,), (0,)), ((), ())), preferred_element_type=jnp.float32)


def folded(product):
    return product[:, :LANES] + product[:, LANES:]


def dense_rows(count, width):
    return count * width // LANES if 4 * width == 3 * LANES and count % 32 == 0 else count


def dense(values, width):
    count = values.shape[0]
    if dense_rows(count, width) == count:
        return values
    rest, side = count // 4, LANES - width
    tail = values[count - rest :, :]
    beside = [tail[:, at : at + side] for at in range(0, width, side)]
    return jnp.concatenate([values[: count - rest, :width], jnp.concatenate(beside, axis=0)], axis=1)


def sparse(values, count, width):
    if dense_rows(count, width) == count:
        return values[:, :width]
    rest = count // 4
    beside = [values[at : at + rest, width:] for at in range(0, count - rest, rest)]
    return jnp.concatenate([values[:, :width], jnp.concatenate(beside, axis=1)], axis=0)


def widened(values):
    room = LANES - values.shape[1]
    return jnp.concatenate([values, jnp.zeros((values.shape[0], room), values.dtype)], axis=1) if room else values


def filter_kernel(n_space, n_orb, degree, start, matrices, node_map, live, lower_list, upper_list, out, gather, scatter, pick, place, stack, raw, node_row, list_row,
                  fields, packed, cell_out, sums, outgoing, arriving, load_sem, send_sem, recv_sem):
    space = lax.axis_index("space")
    width, nodes = start.shape
    cells, doubled, cell_size = stack.shape
    cell_nodes = raw.shape[1]
    whole = cell_nodes // 8 * 8
    tail_at = whole // 16 * 16
    slots = list_row.shape[1] // 2
    list_row[:, :slots] = lower_list[...].astype(jnp.float32)
    list_row[:, slots:] = upper_list[...].astype(jnp.float32)
    count = live[...].astype(jnp.float32)
    for cell in range(cells):
        row = jnp.where(count > float(cell), node_map[cell : cell + 1, :].astype(jnp.float32), -1.0)
        room = cell_size - row.shape[1]
        if room:
            row = jnp.concatenate([row, jnp.full((1, room), -1.0, jnp.float32)], axis=1)
        node_row[:, cell * cell_size : (cell + 1) * cell_size] = row
    has_above, has_below = space < n_space - 1, space > 0

    def load(cell):
        return pltpu.make_async_copy(matrices.at[cell], raw.at[cell % 2], load_sem.at[cell])

    for cell in range(min(cells, 2)):
        load(cell).start()
    arriving[...] = jnp.zeros_like(arriving)

    barrier = pltpu.get_barrier_semaphore()

    @pl.when(has_above)
    def _():
        pl.semaphore_signal(barrier, inc=1, device_id={"space": space + 1}, device_id_type=MESH)

    @pl.when(has_below)
    def _():
        pl.semaphore_signal(barrier, inc=1, device_id={"space": space - 1}, device_id_type=MESH)

    lane = lax.broadcasted_iota(jnp.int32, (LANES, LANES), 1).astype(jnp.float32)
    sublane = lax.broadcasted_iota(jnp.int32, (LANES, LANES), 0).astype(jnp.float32)

    def ones_where(condition):
        return jnp.where(condition, 1.0, 0.0).astype(jnp.bfloat16)

    def tile_at(index):
        return pl.ds(pl.multiple_of(index * LANES, LANES), LANES)

    def upright(row):
        return jnp.transpose(jnp.broadcast_to(row, (LANES, LANES)))

    def gather_rows(chunk, carry):
        here = tile_at(chunk)
        column = upright(node_row[:, here])
        for tile in range(nodes // LANES):
            gather[here, tile * LANES : (tile + 1) * LANES] = ones_where(column == lane + float(tile * LANES))
        return carry

    def pick_rows(chunk, carry):
        here = tile_at(chunk)
        column = upright(list_row[:, here])
        for tile in range(node_row.shape[1] // LANES):
            there = slice(tile * LANES, (tile + 1) * LANES)
            pick[here, there] = ones_where(column == node_row[:, there])
        return carry

    def node_rows(chunk, carry):
        here = tile_at(chunk)
        node = sublane + (chunk * LANES).astype(jnp.float32)
        for tile in range(node_row.shape[1] // LANES):
            there = slice(tile * LANES, (tile + 1) * LANES)
            scatter[here, there] = ones_where(node == node_row[:, there])
        for tile in range(2 * slots // LANES):
            there = slice(tile * LANES, (tile + 1) * LANES)
            other = (tile * LANES + slots) % (2 * slots)
            place[here, there] = ones_where(node == list_row[:, other : other + LANES])
        block = start[:, here]
        if width < LANES:
            block = jnp.concatenate([block, jnp.zeros((LANES - width, LANES), jnp.float32)], axis=0)
        values = jnp.transpose(block)
        fields[0, here, :] = values
        fields[1, here, :] = values
        high, low = split(values)
        packed[here, :LANES] = high
        packed[here, LANES:] = low
        return carry

    lax.fori_loop(0, node_row.shape[1] // LANES, gather_rows, 0)
    for cell in range(cells):
        load(cell).wait()

        def put_split(at, values):
            high, low = split(values)
            stack[cell, pl.ds(at, values.shape[0]), :] = high
            stack[cell, pl.ds(cell_size + at, values.shape[0]), :] = low

        def widen(values):
            room = cell_size - cell_nodes
            return jnp.concatenate([values, jnp.zeros((values.shape[0], room), jnp.float32)], axis=1)

        def split_rows(chunk, carry):
            put_split(pl.multiple_of(chunk * LANES, LANES), widen(raw[cell % 2, tile_at(chunk), :]))
            return carry

        lax.fori_loop(0, tail_at // LANES, split_rows, 0)
        done = tail_at // LANES * LANES
        if tail_at > done:
            put_split(done, widen(raw[cell % 2, done:tail_at, :]))
        if cell_size > tail_at:
            pieces = [widen(raw[cell % 2, tail_at:whole, :])] if whole > tail_at else []
            if cell_nodes > whole:
                row_id = lax.broadcasted_iota(jnp.int32, (8, cell_size), 0)
                block = jnp.zeros((8, cell_size), jnp.float32)
                for row in range(whole, cell_nodes):
                    value = jnp.broadcast_to(widen(raw[cell % 2, row : row + 1, :]), (8, cell_size))
                    block = jnp.where(row_id == row - whole, value, block)
                pieces.append(block)
            room = cell_size - tail_at - sum(piece.shape[0] for piece in pieces)
            if room:
                pieces.append(jnp.zeros((room, cell_size), jnp.float32))
            put_split(tail_at, jnp.concatenate(pieces, axis=0))
        if cell + 2 < cells:
            load(cell + 2).start()
        if cell == 0:
            lax.fori_loop(0, 2 * slots // LANES, pick_rows, 0)
        if cell == min(cells - 1, 1):
            lax.fori_loop(0, nodes // LANES, node_rows, 0)
    pl.semaphore_wait(barrier, has_above.astype(jnp.int32) + has_below.astype(jnp.int32))

    part = nodes // 3 if nodes % (3 * LANES) == 0 else LANES

    def apply(step, carry):
        def one_cell(cell, carry):
            here = pl.ds(pl.multiple_of(cell * cell_size, LANES), cell_size)
            local = plain_dot(gather[here, :], packed[...]).astype(jnp.bfloat16)
            high_part = plain_dot(stack[cell, :cell_size, :], local)
            low_part = plain_dot(stack[cell, cell_size:, :], local[:, :LANES])
            high, low = split(folded(high_part) + low_part)
            cell_out[here, :LANES] = high
            cell_out[here, LANES:] = low
            return carry

        lax.fori_loop(0, cells, one_cell, 0)

        def transfer(way, towards):
            return pltpu.make_async_remote_copy(
                src_ref=outgoing.at[way],
                dst_ref=arriving.at[step, way],
                send_sem=send_sem.at[step, way],
                recv_sem=recv_sem.at[step, way],
                device_id={"space": towards},
                device_id_type=MESH,
            )

        down, up = transfer(0, space - 1), transfer(1, space + 1)
        outgoing[0] = dense(folded(plain_dot(pick[:slots, :], cell_out[...])), width)

        @pl.when(has_below)
        def _():
            down.start()

        outgoing[1] = dense(folded(plain_dot(pick[slots:, :], cell_out[...])), width)

        @pl.when(has_above)
        def _():
            up.start()

        def node_sums(chunk, carry):
            here = pl.ds(pl.multiple_of(chunk * part, LANES), part)
            sums[here, :] = folded(plain_dot(scatter[here, :], cell_out[...]))
            return carry

        lax.fori_loop(0, nodes // part, node_sums, 0)

        @pl.when(has_below)
        def _():
            down.wait_send()
            up.wait_recv()

        @pl.when(has_above)
        def _():
            up.wait_send()
            down.wait_recv()

        new, old = lax.rem(step + 1, 2), lax.rem(step, 2)
        first = step == 0
        scale = jnp.where(first, 1.0 / half_width, 2.0 / half_width)
        keep = jnp.where(first, 0.0, 1.0)
        parts = [split(widened(sparse(arriving[step, way], slots, width))) for way in range(2)]
        arrived = jnp.concatenate([jnp.concatenate(pair, axis=1) for pair in parts], axis=0)

        def advance(chunk, carry):
            here = pl.ds(pl.multiple_of(chunk * part, LANES), part)
            total = sums[here, :] + folded(plain_dot(place[here, :], arrived))
            value = scale * (total - center_shift * fields[old, here, :]) - keep * fields[new, here, :]
            fields[new, here, :] = value
            high, low = split(value)
            packed[here, :LANES] = high
            packed[here, LANES:] = low
            return carry

        lax.fori_loop(0, nodes // part, advance, 0)
        return carry

    lax.fori_loop(0, degree, apply, 0)
    quarter = nodes // n_orb
    for which in range(n_orb):
        out[which] = dense(fields[degree % 2, which * quarter : (which + 1) * quarter, :width], width)


def filtered_block(start, matrices, node_map, live_cells, upper_list, lower_list, n_space, n_orb):
    nodes, width = start.shape
    cells, cell_nodes = node_map.shape
    cell_size = -(-cell_nodes // LANES) * LANES
    slots = upper_list.shape[1]

    sent = dense_rows(nodes // n_orb, width)
    packed_width = LANES if sent != nodes // n_orb else width
    slot_rows = dense_rows(slots, width)
    vmem, anywhere = pl.BlockSpec(memory_space=pltpu.VMEM), pl.BlockSpec(memory_space=pl.ANY)
    dma = pltpu.SemaphoreType.DMA
    every, half = jnp.float32, jnp.bfloat16
    return pl.pallas_call(
        functools.partial(filter_kernel, n_space, n_orb, DEGREE),
        out_shape=jax.ShapeDtypeStruct((n_orb, sent, packed_width), jnp.float32),
        in_specs=[vmem, anywhere, vmem, vmem, vmem, vmem],
        out_specs=vmem,
        scratch_shapes=[
            pltpu.VMEM((cells * cell_size, nodes), half),
            pltpu.VMEM((nodes, cells * cell_size), half),
            pltpu.VMEM((2 * slots, cells * cell_size), half),
            pltpu.VMEM((nodes, 2 * slots), half),
            pltpu.VMEM((cells, 2 * cell_size, cell_size), half),
            pltpu.VMEM((2, cell_nodes, cell_nodes), every),
            pltpu.VMEM((1, cells * cell_size), every),
            pltpu.VMEM((1, 2 * slots), every),
            pltpu.VMEM((2, nodes, LANES), every),
            pltpu.VMEM((nodes, 2 * LANES), half),
            pltpu.VMEM((cells * cell_size, 2 * LANES), half),
            pltpu.VMEM((nodes, LANES), every),
            pltpu.VMEM((2, slot_rows, LANES), every),
            pltpu.VMEM((DEGREE, 2, slot_rows, LANES), every),
            dma((cells,)),
            dma((DEGREE, 2)),
            dma((DEGREE, 2)),
        ],
        compiler_params=pltpu.CompilerParams(
            collective_id=2, has_side_effects=True, vmem_limit_bytes=58 * 2**20
        ),
        name="filter",
    )(jnp.swapaxes(start, 0, 1), matrices, node_map, live_cells, lower_list, upper_list)


def exact_dot(left, right, dims):
    return lax.dot_general(
        left,
        right,
        (dims, ((), ())),
        precision=lax.Precision.HIGHEST,
        preferred_element_type=jnp.float32,
    )


def block_pairs(blocks):
    return [(i, j) for i in range(blocks) for j in range(i + 1)]


def gram_kernel(n_space, n_orb, node_total, inside, field, lower_list, rows_out, gram_out, pieces, local, parts, slab, others,
                turn_send, turn_recv, split_send, split_recv, orb_send, orb_recv, join_send, join_recv):
    space, orb = lax.axis_index("space"), lax.axis_index("orb")
    quarter, columns = rows_out.shape
    width = columns // n_orb
    partners = n_orb - 1

    barrier = pltpu.get_barrier_semaphore()
    for step in range(1, n_orb):
        pl.semaphore_signal(barrier, inc=1, device_id={"orb": lax.rem(orb + step, n_orb)}, device_id_type=MESH)
    if inside:
        partners += n_space - 1
        for step in range(1, n_space):
            pl.semaphore_signal(barrier, inc=1, device_id={"space": lax.rem(space + step, n_space)}, device_id_type=MESH)
    pl.semaphore_wait(barrier, partners)

    def exchange(axis, size, here, send_sems, recv_sems, source, target):
        copies = []
        for step in range(1, size):
            other = lax.rem(here + step, size)
            copy = pltpu.make_async_remote_copy(
                src_ref=source(other),
                dst_ref=target,
                send_sem=send_sems.at[step],
                recv_sem=recv_sems.at[step],
                device_id={axis: other},
                device_id_type=MESH,
            )
            copy.start()
            copies.append(copy)
        return copies

    copies = exchange("orb", n_orb, orb, turn_send, turn_recv, lambda other: field.at[other], pieces.at[orb])
    pieces[orb] = field[orb]
    node = lax.broadcasted_iota(jnp.int32, (quarter, lower_list.shape[1]), 0) + orb * quarter
    hits = jnp.where(node == lower_list[...], 1.0, 0.0)
    weight = (1.0 - jnp.max(hits, axis=1, keepdims=True)) * (1.0 / (n_space * node_total))
    for copy in copies:
        copy.wait()
    for which in range(n_orb):
        rows_out[:, which * width : (which + 1) * width] = sparse(pieces[which], quarter, width)

    blocks = columns // LANES
    for spot, (i, j) in enumerate(block_pairs(blocks)):
        left = rows_out[:, i * LANES : (i + 1) * LANES] * weight
        right = rows_out[:, j * LANES : (j + 1) * LANES]
        term = exact_dot(left, right, ((0,), (0,)))
        if inside:
            local[spot * LANES : (spot + 1) * LANES, :] = term
        else:
            gram_out[spot * LANES : (spot + 1) * LANES, :] = term
    if not inside:
        return

    chunk = local.shape[0] // n_space

    def chunk_of(which):
        return local.at[pl.ds(pl.multiple_of(which * chunk, 8), chunk)]

    copies = exchange("space", n_space, space, split_send, split_recv, chunk_of, parts.at[space])
    parts[space] = local[pl.ds(pl.multiple_of(space * chunk, 8), chunk), :]
    for copy in copies:
        copy.wait()
    slab[...] = jnp.sum(parts[...], axis=0)

    copies = exchange("orb", n_orb, orb, orb_send, orb_recv, lambda _: slab, others.at[orb])
    others[orb] = slab[...]
    for copy in copies:
        copy.wait()
    mine = pl.ds(pl.multiple_of(space * chunk, 8), chunk)
    gram_out[mine, :] = jnp.sum(others[...], axis=0)
    copies = exchange("space", n_space, space, join_send, join_recv, lambda _: gram_out.at[mine], gram_out.at[mine])
    for copy in copies:
        copy.wait()


def turn_and_gram(field, lower_list, node_total, width, n_space, n_orb):
    quarter, columns = node_total // n_orb, width * n_orb
    packed = len(block_pairs(columns // LANES)) * LANES
    inside = n_space <= 8 and packed % (8 * n_space) == 0
    groups = n_space if inside else 1
    chunk = packed // groups
    dma = pltpu.SemaphoreType.DMA
    vmem = pl.BlockSpec(memory_space=pltpu.VMEM)
    rows, gram = pl.pallas_call(
        functools.partial(gram_kernel, n_space, n_orb, node_total, inside),
        out_shape=(
            jax.ShapeDtypeStruct((quarter, columns), jnp.float32),
            jax.ShapeDtypeStruct((packed, LANES), jnp.float32),
        ),
        in_specs=[vmem, vmem],
        out_specs=(vmem, vmem),
        scratch_shapes=[
            pltpu.VMEM(field.shape, jnp.float32),
            pltpu.VMEM((packed, LANES), jnp.float32),
            pltpu.VMEM((groups, chunk, LANES), jnp.float32),
            pltpu.VMEM((chunk, LANES), jnp.float32),
            pltpu.VMEM((n_orb, chunk, LANES), jnp.float32),
            dma((n_orb,)), dma((n_orb,)),
            dma((groups,)), dma((groups,)),
            dma((n_orb,)), dma((n_orb,)),
            dma((groups,)), dma((groups,)),
        ],
        compiler_params=pltpu.CompilerParams(
            collective_id=1, has_side_effects=True, vmem_limit_bytes=40 * 2**20
        ),
        name="turn_and_gram",
    )(field, lower_list)
    if not inside:
        gram = lax.psum(gram, ("space", "orb"))
    return rows, gram


def invert_factor(matrix, inverse):
    size = matrix.shape[0]
    row_id = lax.broadcasted_iota(jnp.int32, (size, size), 0)
    column_id = lax.broadcasted_iota(jnp.int32, (size, size), 1)
    inverse[...] = jnp.where(row_id == column_id, 1.0, 0.0)
    for start in range(0, size, GROUP):
        below = start + GROUP
        rows = [matrix[start + b : start + b + 1, :] for b in range(GROUP)]
        eyes = [inverse[start + b : start + b + 1, :] for b in range(GROUP)]
        entry = {
            (b, c): jnp.broadcast_to(rows[b][:, start + c : start + c + 1], (1, size))
            for b in range(GROUP)
            for c in range(b + 1)
        }
        lower, scale, done = {}, [], []
        for b in range(GROUP):
            scale.append(lax.rsqrt(entry[b, b]))
            for i in range(b + 1, GROUP):
                lower[i, b] = entry[i, b] * scale[b]
            for i in range(b + 1, GROUP):
                for j in range(b + 1, i + 1):
                    entry[i, j] = entry[i, j] - lower[i, b] * lower[j, b]
            done.append((rows[b] * scale[b], eyes[b] * scale[b]))
            for i in range(b + 1, GROUP):
                rows[i] = rows[i] - lower[i, b] * done[b][0]
                eyes[i] = eyes[i] - lower[i, b] * done[b][1]
        for b in range(GROUP):
            inverse[start + b : start + b + 1, :] = done[b][1]
        if below == size:
            break
        back = list(done)
        for b in reversed(range(GROUP)):
            back[b] = (back[b][0] * scale[b], back[b][1] * scale[b])
            for i in range(b):
                back[i] = (back[i][0] - lower[b, i] * back[b][0], back[i][1] - lower[b, i] * back[b][1])
        rest = matrix[below:, :]
        rest_eye = inverse[below:, :]
        raw = [jnp.broadcast_to(rest[:, start + c : start + c + 1], rest.shape) for c in range(GROUP)]
        for c in range(GROUP):
            rest = rest - raw[c] * back[c][0]
            rest_eye = rest_eye - raw[c] * back[c][1]
        matrix[below:, :] = rest
        inverse[below:, :] = rest_eye


def parts_dot(left, right):
    dims = (((1,), (1,)), ((), ()))
    (left_high, left_low), (right_high, right_low) = split(left), split(right)

    def product(a, b):
        return lax.dot_general(a, b, dims, preferred_element_type=jnp.float32)

    return product(left_high, right_high) + (product(left_high, right_low) + product(left_low, right_high))


def rotate_kernel(rows, gram, rotated, lower, block, inverse):
    blocks = rows.shape[1] // LANES
    last = ((1,), (1,))

    def span(k):
        return slice(k * LANES, (k + 1) * LANES)

    for k in range(blocks):
        before = slice(0, k * LANES)
        spot = k * (k + 3) // 2
        diagonal = gram[span(spot), :]
        if k:
            own = lower[k, :, before]
            diagonal = diagonal - exact_dot(own, own, last)
        block[k] = diagonal
        invert_factor(block.at[k], inverse.at[k])
        solved = inverse[k]
        for i in range(k + 1, blocks):
            under = gram[span(i * (i + 1) // 2 + k), :]
            if k:
                under = under - exact_dot(lower[i, :, before], own, last)
            lower[i, :, span(k)] = exact_dot(under, solved, last)
        left = rows[:, span(k)]
        if k:
            left = left - parts_dot(rotated[:, before], own)
        rotated[:, span(k)] = parts_dot(left, solved)


def rotate(rows, gram):
    columns = rows.shape[1]
    vmem = pl.BlockSpec(memory_space=pltpu.VMEM)
    return pl.pallas_call(
        rotate_kernel,
        out_shape=jax.ShapeDtypeStruct(rows.shape, jnp.float32),
        in_specs=[vmem, vmem],
        out_specs=vmem,
        scratch_shapes=[
            pltpu.VMEM((columns // LANES, LANES, columns), jnp.float32),
            pltpu.VMEM((columns // LANES, LANES, LANES), jnp.float32),
            pltpu.VMEM((columns // LANES, LANES, LANES), jnp.float32),
        ],
        compiler_params=pltpu.CompilerParams(vmem_limit_bytes=40 * 2**20),
        name="rotate",
    )(rows, gram)


def shards(wavefunctions, cell_ham, cell_nodes, cell_count, upper_nodes, lower_nodes):
    n_space, n_orb = lax.axis_size("space"), lax.axis_size("orb")
    current = filtered_block(
        wavefunctions[0], cell_ham[0], cell_nodes[0], cell_count[:, None], upper_nodes, lower_nodes,
        n_space, n_orb,
    )
    rows, gram = turn_and_gram(current, lower_nodes, *wavefunctions.shape[1:], n_space, n_orb)
    return rotate(rows, gram)[None]


def solution(mesh):
    in_specs = (
        P("space", None, "orb"),
        P("space", None, None, None),
        P("space", None, None),
        P("space"),
        P("space", None),
        P("space", None),
    )
    out_specs = P("space", "orb", None)
    return jax.shard_map(shards, mesh=mesh, in_specs=in_specs, out_specs=out_specs, check_vma=False)
```
